256 devices in a mesh: dp: 32 (over y_lo, z, core), section: 8 (over y_hi, x).
Axes of the slice: x: 4, y: 4 (y_hi: 2, y_lo: 2; y = y_hi * 2 + y_lo), z: 8, core: 2. Of those that a mesh axis runs over, the one named last changes fastest.
Arguments:
- inputs: bfloat16 [32, 512, 1536], P('dp', 'section'), may hold values from -36 to 36
- lengths: int32 [32], P('dp'), may hold values from 1 to 512, 10240 in all
- cotangent: bfloat16 [32, 512, 1536], P('dp', 'section'), may hold values from -6 to 6
- weight: bfloat16 [8, 1536, 1536], P('section'), may hold values from -0.15625 to 0.15625
- kern: float32 [8, 15, 1536], P('section'), may hold values from -1.5 to 1.5
- gain: float32 [8, 1536], P('section'), may hold values from 0.1 to 1.9
Outputs:
- outputs: bfloat16 [32, 512, 1536], P('dp', 'section')
- input_grad: bfloat16 [32, 512, 1536], P('dp', 'section')
- weight_grad: float32 [8, 1536, 1536], P('section', 'dp')
- kernel_grad: float32 [8, 15, 1536], P('section')
- gain_grad: float32 [8, 1536], P('section')
The draws below stay inside these ranges and needn't reach their ends.
Inputs may be any that keep to these rules, and one draw needn't show every extreme that they name: `lengths`: each utterance's number of valid frames; frames from it on are padding. Some utterance is whole in every draw.
All inputs are finite; a program needn't handle non-finite values. No bound on the sum of `lengths` on one device may be relied on, other than what follows from the above.
Results may differ from the reference program's by a relative error of at most 0.034.
Values may be sent and summed in bfloat16 or wider, within the bound.
A program may use at most 64 MiB of HBM per device.

```python
import math
import jax
import jax.numpy as jnp
import numpy as np
from jax import lax

D = 1536
TAPS = 15
FRAMES = 512
UTT = 32
LAYERS = 8


def draw_inputs(key, part):
    key = jax.random.fold_in(key, 11)
    first, second, third = jax.random.split(key, 3)
    row_scale = jnp.exp(jax.random.uniform(second, (UTT, FRAMES, 1), jnp.float32, math.log(0.3), math.log(3.0)))
    col_scale = jnp.exp(jax.random.uniform(third, (1, 1, D), jnp.float32, math.log(0.3), math.log(3.0)))
    base = jnp.clip(jax.random.normal(first, (UTT, FRAMES, D), jnp.float32), -4.0, 4.0)
    return (base * row_scale * col_scale).astype(jnp.bfloat16)


def spiked(array, stream_key, source, target, parts, factor):
    def block_of(axis_at):
        return (jnp.arange(array.shape[axis_at]) // (array.shape[axis_at] // parts)).reshape((-1,) + (1,) * (array.ndim - 1 - axis_at))

    one_side = jax.random.permutation(stream_key, parts)[block_of(target)]
    second = (block_of(target) + parts // 2) % parts
    return jnp.where((block_of(source) == one_side) | (block_of(source) == second), factor * array, array)


def shard_levels(rng, shape, cuts, smallest, top_value):
    loudness = 1.0
    for position, shards_of in cuts:
        steps = jax.random.uniform(jax.random.fold_in(jax.random.fold_in(rng, 6), position), (shards_of,), jnp.float32, smallest / len(cuts), top_value / len(cuts))
        loudness = loudness * jnp.repeat(jnp.exp(steps), shape[position] // shards_of).reshape((-1,) + (1,) * (len(shape) - 1 - position))
    return loudness


def profile(number_of, total, most, slope):
    loads = [(1 << 20) // math.isqrt(rank ** slope) + 1 for rank in range(2, number_of + 1)]
    spare, given = total - most - (number_of - 1), [1] * (number_of - 1)
    while spare > 0:
        candidates = [i for i in range(number_of - 1) if given[i] < most]
        pool, remaining = sum([loads[i] for i in candidates]), spare
        for i in candidates:
            extra = min(most - given[i], max(1, remaining * loads[i] // pool), spare)
            given[i] = given[i] + extra
            spare = spare - extra
    return np.array([most] + given)


def uneven(own_key, amount, total, limit, lean):
    if amount == 2:
        one = jax.random.randint(own_key, (), max(1, total - limit), min(limit, total - 1) + 1)
        return jnp.stack([one, total - one])
    tallies = jnp.asarray(profile(amount, total, limit, lean), jnp.int32)
    twos = (amount - 1) // 2
    giver, receiver = tallies[1:1 + 2 * twos:2], tallies[2:2 + 2 * twos:2]
    room = jnp.minimum(giver - 1, limit - receiver)
    passed = jax.random.randint(jax.random.fold_in(own_key, 1), (twos,), 0, 1 << 20) % (room + 1)
    tallies = tallies.at[1:1 + 2 * twos:2].set(giver - passed).at[2:2 + 2 * twos:2].set(receiver + passed)
    return tallies[jax.random.permutation(jax.random.fold_in(own_key, 2), amount)]


def noise(rng, shape, width, most, shards=(), held_as=jnp.bfloat16):
    factor_of = shard_levels(rng, shape, shards, -0.22, 0.18) if shards else 1.0
    values = jax.random.normal(rng, shape, jnp.float32) * width * factor_of
    return jnp.minimum(jnp.maximum(values, -most), most).astype(held_as)


def gaussian_with(own_key, dims, width, reach, pieces, heavy, kind=jnp.bfloat16):
    values = width * jax.random.normal(own_key, dims, jnp.float32)
    if pieces:
        values = values * shard_levels(own_key, dims, pieces, -0.22, 0.18)
    return jnp.clip(spiked(values, jax.random.fold_in(own_key, 3), *heavy), -reach, reach).astype(kind)


def setup_inputs(seed: int = 0) -> dict:
    streams_of = jax.random.split(jax.random.key(seed), 7)
    return {
        "inputs": draw_inputs(jax.random.fold_in(streams_of[6], 71), 0),
        "lengths": uneven(streams_of[1], UTT, UTT * FRAMES * 5 // 8, FRAMES, 1).astype(jnp.int32),
        "cotangent": gaussian_with(streams_of[2], (UTT, FRAMES, D), 1.0, 6.0, ((0, 32), (1, 8)), (0, 2, 32, 2.75)),
        "weight": noise(streams_of[3], (LAYERS, D, D), D ** -0.5, 0.15625, ((0, 8),)),
        "kern": noise(streams_of[4], (LAYERS, TAPS, D), TAPS ** -0.5, 1.5, ((0, 8),), jnp.float32),
        "gain": jnp.clip(1.0 + 0.18 * jax.random.normal(streams_of[5], (LAYERS, D), jnp.float32), 0.1, 1.9),
    }


epsilon = 1e-05

def silu_slope(value):
    sigma = jax.nn.sigmoid(value)
    return sigma * (1.0 + value * (1.0 - sigma))

def causal_mix(padded, taps, frame_total):
    total = taps[0] * padded[0:frame_total]
    for k in range(1, taps.shape[0]):
        total = total + taps[k] * padded[k:k + frame_total]
    return total

def layer_parts(stream, taps, gain_row, context_len, frame_total):
    wide = stream.astype(jnp.float32)
    inverse_rms = lax.rsqrt(lax.optimization_barrier(jnp.mean(wide * wide, axis=1, keepdims=True)) + epsilon)
    scaled = wide * inverse_rms
    normed = scaled * gain_row
    padded = jnp.pad(normed, ((context_len, 0), (0, 0)))
    mixed_conv = causal_mix(padded, taps, frame_total)
    activated = jax.nn.silu(mixed_conv).astype(jnp.bfloat16)
    return (wide, inverse_rms, scaled, padded, mixed_conv, activated)

def utterance_pass(stream_in, grad_in, length, weight, kern, gain):
    frame_total = stream_in.shape[0]
    context_len = kern.shape[1] - 1
    valid = (jnp.arange(frame_total, dtype=jnp.int32) < length)[:, None]
    history = []
    stream = stream_in
    for layer in range(LAYERS):
        history.append(stream)
        wide, inverse_rms, scaled, padded, mixed_conv, activated = layer_parts(stream, kern[layer], gain[layer], context_len, frame_total)
        projected = lax.dot_general(activated, weight[layer], (((1,), (1,)), ((), ())), preferred_element_type=jnp.float32)
        stream = (wide + jnp.where(valid, projected, 0.0)).astype(jnp.bfloat16)
    grad = grad_in
    weight_terms = []
    kernel_terms = []
    gain_terms = []
    for layer in range(LAYERS - 1, -1, -1):
        wide, inverse_rms, scaled, padded, mixed_conv, activated = layer_parts(history[layer], kern[layer], gain[layer], context_len, frame_total)
        grad_p = jnp.where(valid, grad, jnp.zeros_like(grad))
        weight_terms.append(lax.dot_general(grad_p, activated, (((0,), (0,)), ((), ())), preferred_element_type=jnp.float32))
        grad_a = jnp.dot(grad_p, weight[layer], preferred_element_type=jnp.float32)
        grad_c = grad_a * silu_slope(mixed_conv)
        grad_pad = jnp.pad(grad_c, ((0, context_len), (0, 0)))
        taps = kern[layer]
        grad_n = taps[0] * grad_pad[context_len:context_len + frame_total]
        for k in range(1, taps.shape[0]):
            grad_n = grad_n + taps[k] * grad_pad[context_len - k:context_len - k + frame_total]
        kernel_terms.append(jnp.stack([lax.optimization_barrier(jnp.sum(grad_c * padded[k:k + frame_total], axis=0)) for k in range(taps.shape[0])]))
        gain_terms.append(lax.optimization_barrier(jnp.sum(grad_n * scaled, axis=0)))
        gh_scaled = grad_n * gain[layer]
        grad_h = inverse_rms * (gh_scaled - scaled * lax.optimization_barrier(jnp.mean(gh_scaled * scaled, axis=1, keepdims=True)))
        grad = (grad.astype(jnp.float32) + grad_h).astype(jnp.bfloat16)
    return (stream, grad, jnp.stack(weight_terms[::-1]), jnp.stack(kernel_terms[::-1]), jnp.stack(gain_terms[::-1]))

def reference(inputs, lengths, cotangent, weight, kern, gain):

    def visit(totals, item):
        stream_in, grad_in, length = item
        result, grad, w_terms, k_terms, g_terms = utterance_pass(stream_in, grad_in, length, weight, kern, gain)
        return ((totals[0] + w_terms, totals[1] + k_terms, totals[2] + g_terms), (result, grad))
    start_sums = (jnp.zeros((LAYERS, D, D), jnp.float32), jnp.zeros((LAYERS, TAPS, D), jnp.float32), jnp.zeros((LAYERS, D), jnp.float32))
    totals, pairs = lax.scan(visit, start_sums, (inputs, cotangent, lengths))
    return (pairs[0], pairs[1], totals[0], totals[1], totals[2])
```

```python
import functools

import jax
import jax.numpy as jnp
from jax import lax
from jax.experimental import pallas as pl
from jax.experimental.pallas import tpu as pltpu
from jax.sharding import PartitionSpec as P

EPSILON = 1e-05
BLOCK = 32
COLUMNS = 256
CHUNK = 512
F32 = jnp.float32
BF16 = jnp.bfloat16


def order_matrix(frames, block, back):
    groups = block // 8
    row = lax.broadcasted_iota(jnp.int32, (frames, frames), 0)
    col = lax.broadcasted_iota(jnp.int32, (frames, frames), 1)
    kept, time = (col, row) if back else (row, col)
    inside = lax.rem(kept, block)
    frame = kept - inside + groups * lax.rem(inside, 8) + lax.div(inside, 8)
    return (frame == time).astype(BF16)


def kernel(
    sections, frames, taps, n_block,
    x_ref, len_ref, cot_ref, w_hbm, kern_ref, gain_ref,
    out_ref, igrad_ref, wg_ref, small_ref,
    w, hist, hout, normed, slope, act, inv, gin, gout, gp, gc, gh, kb, kacc, gacc, xin, cin, orecv, irecv,
    w_sem, f_recv, f_send, b_recv, b_send, x_send, c_send, o_recv, i_recv,
):
    me = lax.axis_index("section")
    last = sections - 1
    feature = x_ref.shape[1]
    per = frames // BLOCK
    groups = BLOCK // 8
    halo = taps - 1

    w_copy = pltpu.make_async_copy(w_hbm, w, w_sem)
    w_copy.start()

    barrier = pltpu.get_barrier_semaphore()
    for d in range(1, sections):
        pl.semaphore_signal(
            barrier, inc=1, device_id={"section": lax.rem(me + d, sections)}, device_id_type=pl.DeviceIdType.MESH
        )

    to_kept = order_matrix(frames, BLOCK, False)
    xin[...] = jnp.dot(to_kept, x_ref[...], preferred_element_type=F32).astype(BF16).reshape(xin.shape)
    cin[...] = jnp.dot(to_kept, cot_ref[...], preferred_element_type=F32).astype(BF16).reshape(cin.shape)

    for k in range(taps):
        kb[k] = jnp.broadcast_to(kern_ref[k : k + 1, :], (8, feature))
    kb[taps] = jnp.broadcast_to(gain_ref[...], (8, feature))
    normed[0] = jnp.zeros_like(normed[0])
    gc[n_block] = jnp.zeros_like(gc[n_block])
    kacc[...] = jnp.zeros_like(kacc)
    gacc[...] = jnp.zeros_like(gacc)

    @pl.when(me == 0)
    def _():
        for i in range(per):
            hist[i] = xin[i]

    @pl.when(me == last)
    def _():
        for i in range(per):
            gin[n_block - per + i] = cin[i]

    pl.semaphore_wait(barrier, sections - 1)

    def send(src, dst, send_sem, recv_sem, to):
        return pltpu.make_async_remote_copy(
            src_ref=src, dst_ref=dst, send_sem=send_sem, recv_sem=recv_sem,
            device_id={"section": to}, device_id_type=pl.DeviceIdType.MESH,
        )

    def x_copy(i):
        return send(xin.at[i], hist.at[me * per + i], x_send, f_recv.at[me * per + i], 0)

    def c_copy(i):
        return send(cin.at[i], gin.at[me * per + i], c_send, b_recv.at[me * per + i], last)

    @pl.when(me != 0)
    def _():
        for i in range(per):
            x_copy(i).start()

    @pl.when(me != last)
    def _():
        for i in reversed(range(per)):
            c_copy(i).start()

    sub = lax.broadcasted_iota(jnp.int32, (8, COLUMNS), 0)
    length = len_ref[0]

    def valid_rows(b):
        row = lax.broadcasted_iota(jnp.int32, (BLOCK, 1), 0)
        frame = b * BLOCK + groups * lax.rem(row, 8) + lax.div(row, 8)
        return frame < length

    def cols_of(c):
        return pl.ds(pl.multiple_of(c * COLUMNS, COLUMNS), COLUMNS)

    def forward(b, carry):
        @pl.when((me != 0) | (b >= per))
        def _():
            send(hist.at[b], hist.at[b], f_send.at[b], f_recv.at[b], 0).wait_recv()

        wide = hist[b].astype(F32)
        inverse = lax.rsqrt(jnp.sum(wide * wide, axis=1, keepdims=True) * (1.0 / feature) + EPSILON)
        inv[b] = jnp.broadcast_to(inverse, (BLOCK, 128))
        normed[b + 1] = (wide * inverse) * gain_ref[...]

        def column(c, carry):
            cols = cols_of(c)
            now = [normed[b + 1, 8 * r : 8 * r + 8, cols] for r in range(groups)]
            past = [normed[b, 8 * r : 8 * r + 8, cols] for r in range(groups)]
            shifted = {r: now[r] for r in range(groups)}
            for m in range(1, halo + 1):
                q = -(-m // groups)
                r = q * groups - m
                shifted[-m] = pltpu.roll(jnp.where(sub >= 8 - q, past[r], now[r]), q, 0)
            total = [None] * groups
            for k in range(taps):
                tap = kb[k, :, cols]
                for r in range(groups):
                    term = tap * shifted[r - halo + k]
                    total[r] = term if k == 0 else total[r] + term
            for r in range(0, groups, 2):
                acts = []
                for h in (r, r + 1):
                    v = total[h]
                    s = 0.5 * jnp.tanh(0.5 * v) + 0.5
                    a = v * s
                    slope[b, 8 * h : 8 * h + 8, cols] = s + a * (1.0 - s)
                    acts.append(a)
                act[b, 8 * r : 8 * r + 16, cols] = jnp.concatenate(acts, axis=0).astype(BF16)
            return carry

        lax.fori_loop(0, feature // COLUMNS, column, 0)

        valid = valid_rows(b)
        a = act[b]
        to = jnp.minimum(me + 1, last)
        holder = lax.div(b, per)
        for n in range(0, feature, CHUNK):
            part = lax.dot_general(
                a, w[n : n + CHUNK, :], (((1,), (1,)), ((), ())), preferred_element_type=F32
            )
            res = hist[b, :, n : n + CHUNK].astype(F32) + jnp.where(valid, part, 0.0)
            hout[b, :, n : n + CHUNK] = res.astype(BF16)

            @pl.when(me != last)
            def _():
                send(
                    hout.at[b, :, pl.ds(n, CHUNK)], hist.at[b, :, pl.ds(n, CHUNK)], f_send.at[b], f_recv.at[b], to
                ).start()

        @pl.when((me == last) & (holder != last))
        def _():
            send(hout.at[b], orecv.at[lax.rem(b, per)], f_send.at[b], o_recv.at[lax.rem(b, per)], holder).start()

        return carry

    w_copy.wait()
    lax.fori_loop(0, n_block, forward, 0)

    from_kept = order_matrix(frames, BLOCK, True)

    def give(ref, rows):
        ref[...] = jnp.dot(from_kept, rows.reshape(frames, feature), preferred_element_type=F32).astype(BF16)

    @pl.when(me != last)
    def _():
        for i in range(per):
            send(orecv.at[i], orecv.at[i], f_send.at[i], o_recv.at[i], 0).wait_recv()
        give(out_ref, orecv[...])

    def backward(step, carry):
        b = n_block - 1 - step

        @pl.when((me != last) | (b < n_block - per))
        def _():
            send(gin.at[b], gin.at[b], b_send.at[b], b_recv.at[b], 0).wait_recv()

        g = gin[b]
        masked = jnp.where(valid_rows(b), g.astype(F32), 0.0).astype(BF16)
        gp[b] = masked
        for n in range(0, feature, CHUNK):
            ga = jnp.dot(masked, w[:, n : n + CHUNK], preferred_element_type=F32)
            gc[b, :, n : n + CHUNK] = ga * slope[b, :, n : n + CHUNK]

        inverse = [inv[b, 8 * r : 8 * r + 8, 0:1] for r in range(groups)]

        def scaled_of(cols):
            rows = hist[b, :, cols].astype(F32)
            return [rows[8 * r : 8 * r + 8] * inverse[r] for r in range(groups)]

        def column(c, sums):
            cols = cols_of(c)
            now = [gc[b, 8 * r : 8 * r + 8, cols] for r in range(groups)]
            later = [gc[b + 1, 8 * r : 8 * r + 8, cols] for r in range(groups)]
            shifted = {r: now[r] for r in range(groups)}
            for e in range(groups, groups + halo):
                q, r = divmod(e, groups)
                shifted[e] = pltpu.roll(jnp.where(sub < q, later[r], now[r]), 8 - q, 0)
            base = [normed[b + 1, 8 * r : 8 * r + 8, cols] for r in range(groups)]
            total = [None] * groups
            for k in range(taps):
                tap = kb[k, :, cols]
                grown = kacc[k, :, cols]
                for r in range(groups):
                    value = shifted[r + halo - k]
                    term = tap * value
                    total[r] = term if k == 0 else total[r] + term
                    grown = grown + value * base[r]
                kacc[k, :, cols] = grown
            scaled = scaled_of(cols)
            gain = kb[taps, :, cols]
            grown = gacc[:, cols]
            sums = list(sums)
            for r in range(groups):
                product = total[r] * scaled[r]
                grown = grown + product
                gh[8 * r : 8 * r + 8, cols] = total[r] * gain
                product = product * gain
                for p in range(0, COLUMNS, 128):
                    sums[r] = sums[r] + product[:, p : p + 128]
            gacc[:, cols] = grown
            return tuple(sums)

        sums = lax.fori_loop(
            0, feature // COLUMNS, column, tuple(jnp.zeros((8, 128), F32) for _ in range(groups))
        )
        means = jnp.concatenate([jnp.sum(s, axis=1, keepdims=True) for s in sums], axis=0) * (1.0 / feature)
        inverse_all = inv[b, :, 0:1]
        to = jnp.maximum(me - 1, 0)
        holder = lax.div(b, per)
        for n in range(0, feature, CHUNK):
            cols = slice(n, n + CHUNK)
            scaled = hist[b, :, cols].astype(F32) * inverse_all
            grad_h = inverse_all * (gh[:, cols] - scaled * means)
            gout[b, :, cols] = (gin[b, :, cols].astype(F32) + grad_h).astype(BF16)

            @pl.when(me != 0)
            def _():
                send(
                    gout.at[b, :, pl.ds(n, CHUNK)], gin.at[b, :, pl.ds(n, CHUNK)], b_send.at[b], b_recv.at[b], to
                ).start()

        @pl.when((me == 0) & (holder != 0))
        def _():
            send(gout.at[b], irecv.at[lax.rem(b, per)], b_send.at[b], i_recv.at[lax.rem(b, per)], holder).start()

        return carry

    lax.fori_loop(0, n_block, backward, 0)

    @pl.when(me == last)
    def _():
        give(out_ref, hout[n_block - per : n_block])

    @pl.when(me == 0)
    def _():
        give(igrad_ref, gout[0:per])

    small_ref[0:taps, :] = jnp.sum(kacc[...], axis=1)
    small_ref[taps : taps + 1, :] = jnp.sum(gacc[...], axis=0, keepdims=True)

    def weight_rows(o, carry):
        rows = pl.ds(pl.multiple_of(o * COLUMNS, COLUMNS), COLUMNS)
        left = gp[:, :, rows].reshape(n_block * BLOCK, COLUMNS)
        right = act[...].reshape(n_block * BLOCK, feature)
        wg_ref[rows, :] = lax.dot_general(
            left, right, (((0,), (0,)), ((), ())), preferred_element_type=F32
        ).astype(BF16)
        return carry

    lax.fori_loop(0, feature // COLUMNS, weight_rows, 0)

    @pl.when(me != 0)
    def _():
        for i in range(per):
            send(irecv.at[i], irecv.at[i], b_send.at[i], i_recv.at[i], 0).wait_recv()
        give(igrad_ref, irecv[...])

    @pl.when(me != 0)
    def _():
        send(xin, xin, x_send, o_recv.at[0], 0).wait_send()

    @pl.when(me != last)
    def _():
        send(cin, cin, c_send, o_recv.at[0], 0).wait_send()

    def sent(b, carry):
        @pl.when((me != last) | (b < n_block - per))
        def _():
            send(hout.at[b], hist.at[b], f_send.at[b], f_recv.at[b], 0).wait_send()

        @pl.when((me != 0) | (b >= per))
        def _():
            send(gout.at[b], gin.at[b], b_send.at[b], b_recv.at[b], 0).wait_send()

        return carry

    lax.fori_loop(0, n_block, sent, 0)


def pipeline(x, lengths, cot, weight, kern, gain):
    sections = lax.axis_size("section")
    frames, feature = x.shape
    taps = kern.shape[0]
    n_block = sections * frames // BLOCK
    per = frames // BLOCK
    vmem = pl.BlockSpec(memory_space=pltpu.VMEM)
    blocks = (n_block, BLOCK, feature)
    own = (per, BLOCK, feature)
    return pl.pallas_call(
        functools.partial(kernel, sections, frames, taps, n_block),
        out_shape=(
            jax.ShapeDtypeStruct((frames, feature), BF16),
            jax.ShapeDtypeStruct((frames, feature), BF16),
            jax.ShapeDtypeStruct((feature, feature), BF16),
            jax.ShapeDtypeStruct((taps + 1, feature), F32),
        ),
        in_specs=[
            vmem, pl.BlockSpec(memory_space=pltpu.SMEM), vmem, pl.BlockSpec(memory_space=pl.ANY), vmem, vmem,
        ],
        out_specs=(vmem, vmem, vmem, vmem),
        scratch_shapes=[
            pltpu.VMEM((feature, feature), BF16),
            pltpu.VMEM(blocks, BF16),
            pltpu.VMEM(blocks, BF16),
            pltpu.VMEM((n_block + 1, BLOCK, feature), F32),
            pltpu.VMEM(blocks, F32),
            pltpu.VMEM(blocks, BF16),
            pltpu.VMEM((n_block, BLOCK, 128), F32),
            pltpu.VMEM(blocks, BF16),
            pltpu.VMEM(blocks, BF16),
            pltpu.VMEM(blocks, BF16),
            pltpu.VMEM((n_block + 1, BLOCK, feature), F32),
            pltpu.VMEM((BLOCK, feature), F32),
            pltpu.VMEM((taps + 1, 8, feature), F32),
            pltpu.VMEM((taps, 8, feature), F32),
            pltpu.VMEM((8, feature), F32),
            pltpu.VMEM(own, BF16),
            pltpu.VMEM(own, BF16),
            pltpu.VMEM(own, BF16),
            pltpu.VMEM(own, BF16),
            pltpu.SemaphoreType.DMA,
            pltpu.SemaphoreType.DMA((n_block,)),
            pltpu.SemaphoreType.DMA((n_block,)),
            pltpu.SemaphoreType.DMA((n_block,)),
            pltpu.SemaphoreType.DMA((n_block,)),
            pltpu.SemaphoreType.DMA,
            pltpu.SemaphoreType.DMA,
            pltpu.SemaphoreType.DMA((per,)),
            pltpu.SemaphoreType.DMA((per,)),
        ],
        compiler_params=pltpu.CompilerParams(
            collective_id=0, has_side_effects=True, vmem_limit_bytes=60 * 1024 * 1024
        ),
        cost_estimate=pl.CostEstimate(
            flops=6 * n_block * BLOCK * feature * feature, bytes_accessed=4 * feature * feature, transcendentals=0
        ),
    )(x, lengths, cot, weight, kern, gain)


def local(inputs, lengths, cotangent, weight, kern, gain):
    out, igrad, wg, small = pipeline(inputs[0], lengths, cotangent[0], weight[0], kern[0], gain)
    weight_rows = lax.psum_scatter(wg, "dp", scatter_dimension=0, tiled=True).astype(F32)
    total = lax.psum(small.astype(BF16), "dp").astype(F32)
    taps = kern.shape[1]
    return (out[None], igrad[None], weight_rows[None], total[None, :taps], total[taps:])


def solution(mesh):
    return jax.shard_map(
        local,
        mesh=mesh,
        in_specs=(
            P("dp", "section", None),
            P("dp"),
            P("dp", "section", None),
            P("section", None, None),
            P("section", None, None),
            P("section", None),
        ),
        out_specs=(
            P("dp", "section", None),
            P("dp", "section", None),
            P("section", "dp", None),
            P("section", None, None),
            P("section", None),
        ),
        check_vma=False,
    )
```

```python
import functools

import jax
import jax.numpy as jnp
from jax import lax
from jax.experimental import pallas as pl
from jax.experimental.pallas import tpu as pltpu
from jax.sharding import PartitionSpec as P

EPSILON = 1e-05
BLOCK = 32
COLUMNS = 256
CHUNK = 512
F32 = jnp.float32
BF16 = jnp.bfloat16


def order_matrix(frames, block, back):
    groups = block // 8
    row = lax.broadcasted_iota(jnp.int32, (frames, frames), 0)
    col = lax.broadcasted_iota(jnp.int32, (frames, frames), 1)
    kept, time = (col, row) if back else (row, col)
    inside = lax.rem(kept, block)
    frame = kept - inside + groups * lax.rem(inside, 8) + lax.div(inside, 8)
    return (frame == time).astype(BF16)


RING = 8
HALF = 4


def kernel(
    sections, frames, taps, n_block,
    x_ref, len_ref, cot_ref, w_hbm, kern_ref, gain_ref,
    out_ref, igrad_ref, wg_ref, kgrad_ref, ggrad_ref,
    w, wt, hist, hout, normed, slope, act, inv, gin, gout, gp, gc, gh, kb, kacc, gacc, xin, cin, orecv, irecv,
    wgl, core_in, z_out, z_in, y_out, y_in, last_out, last_in, s_own, s_core, s_half, s_y, s_z, s_fin, s_got, s_back,
    w_sem, f_recv, f_send, b_recv, b_send, x_send, c_send, o_recv, i_recv,
    wg_send, wg_recv, z_send, z_recv, y_send, y_recv, last_sem, s_send, s_recv,
):
    me = lax.axis_index("section")
    last = sections - 1
    feature = x_ref.shape[1]
    per = frames // BLOCK
    groups = BLOCK // 8
    halo = taps - 1

    w_copy = pltpu.make_async_copy(w_hbm, w, w_sem)
    w_copy.start()

    dp = lax.axis_index("dp")
    core = lax.rem(dp, 2)
    z = lax.rem(lax.div(dp, 2), RING)
    y = lax.div(dp, 2 * RING)

    def around(offset):
        return lax.rem(z + offset + RING, RING)

    def peer(y_at, z_at, core_at):
        return {"dp": (y_at * RING + z_at) * 2 + core_at}

    other_core = peer(y, z, 1 - core)
    other_y = peer(1 - y, z, core)

    barrier = pltpu.get_barrier_semaphore()
    partners = [{"section": lax.rem(me + d, sections)} for d in range(1, sections)]
    partners += [peer(y, around(d), core) for d in range(1, RING)] + [other_core, other_y]
    for partner in partners:
        pl.semaphore_signal(barrier, inc=1, device_id=partner, device_id_type=pl.DeviceIdType.MESH)

    to_kept = order_matrix(frames, BLOCK, False)
    xin[...] = jnp.dot(to_kept, x_ref[...], preferred_element_type=F32).astype(BF16).reshape(xin.shape)
    cin[...] = jnp.dot(to_kept, cot_ref[...], preferred_element_type=F32).astype(BF16).reshape(cin.shape)

    for k in range(taps):
        kb[k] = jnp.broadcast_to(kern_ref[k : k + 1, :], (8, feature))
    kb[taps] = jnp.broadcast_to(gain_ref[...], (8, feature))
    normed[0] = jnp.zeros_like(normed[0])
    gc[n_block] = jnp.zeros_like(gc[n_block])
    kacc[...] = jnp.zeros_like(kacc)
    gacc[...] = jnp.zeros_like(gacc)

    @pl.when(me == 0)
    def _():
        for i in range(per):
            hist[i] = xin[i]

    @pl.when(me == last)
    def _():
        for i in range(per):
            gin[n_block - per + i] = cin[i]

    w_copy.wait()

    def turn(i, carry):
        strip = pl.ds(pl.multiple_of(i * COLUMNS, COLUMNS), COLUMNS)
        wt[:, strip] = w[strip, :].T
        return carry

    lax.fori_loop(0, feature // COLUMNS, turn, 0)
    pl.semaphore_wait(barrier, len(partners))

    def send(src, dst, send_sem, recv_sem, to):
        return pltpu.make_async_remote_copy(
            src_ref=src, dst_ref=dst, send_sem=send_sem, recv_sem=recv_sem,
            device_id=to if isinstance(to, dict) else {"section": to}, device_id_type=pl.DeviceIdType.MESH,
        )

    def x_copy(i):
        return send(xin.at[i], hist.at[me * per + i], x_send, f_recv.at[me * per + i], 0)

    def c_copy(i):
        return send(cin.at[i], gin.at[me * per + i], c_send, b_recv.at[me * per + i], last)

    @pl.when(me != 0)
    def _():
        for i in range(per):
            x_copy(i).start()

    @pl.when(me != last)
    def _():
        for i in reversed(range(per)):
            c_copy(i).start()

    sub = lax.broadcasted_iota(jnp.int32, (8, COLUMNS), 0)
    length = len_ref[0]

    def valid_rows(b):
        row = lax.broadcasted_iota(jnp.int32, (BLOCK, 1), 0)
        frame = b * BLOCK + groups * lax.rem(row, 8) + lax.div(row, 8)
        return frame < length

    def cols_of(c):
        return pl.ds(pl.multiple_of(c * COLUMNS, COLUMNS), COLUMNS)

    def forward(b, carry):
        @pl.when((me != 0) | (b >= per))
        def _():
            send(hist.at[b], hist.at[b], f_send.at[b], f_recv.at[b], 0).wait_recv()

        wide = hist[b].astype(F32)
        inverse = lax.rsqrt(jnp.sum(wide * wide, axis=1, keepdims=True) * (1.0 / feature) + EPSILON)
        inv[b] = jnp.broadcast_to(inverse, (BLOCK, 128))
        normed[b + 1] = (wide * inverse) * gain_ref[...]

        def column(c, carry):
            cols = cols_of(c)
            now = [normed[b + 1, 8 * r : 8 * r + 8, cols] for r in range(groups)]
            past = [normed[b, 8 * r : 8 * r + 8, cols] for r in range(groups)]
            shifted = {r: now[r] for r in range(groups)}
            for m in range(1, halo + 1):
                q = -(-m // groups)
                r = q * groups - m
                shifted[-m] = pltpu.roll(jnp.where(sub >= 8 - q, past[r], now[r]), q, 0)
            total = [None] * groups
            for k in range(taps):
                tap = kb[k, :, cols]
                for r in range(groups):
                    term = tap * shifted[r - halo + k]
                    total[r] = term if k == 0 else total[r] + term
            for r in range(0, groups, 2):
                acts = []
                for h in (r, r + 1):
                    v = total[h]
                    s = 0.5 * jnp.tanh(0.5 * v) + 0.5
                    a = v * s
                    slope[b, 8 * h : 8 * h + 8, cols] = s + a * (1.0 - s)
                    acts.append(a)
                act[b, 8 * r : 8 * r + 16, cols] = jnp.concatenate(acts, axis=0).astype(BF16)
            return carry

        lax.fori_loop(0, feature // COLUMNS, column, 0)

        valid = valid_rows(b)
        a = act[b]
        to = jnp.minimum(me + 1, last)
        holder = lax.div(b, per)
        for n in range(0, feature, CHUNK):
            part = lax.dot_general(
                a, wt[:, n : n + CHUNK], (((1,), (0,)), ((), ())), preferred_element_type=F32
            )
            res = hist[b, :, n : n + CHUNK].astype(F32) + jnp.where(valid, part, 0.0)
            hout[b, :, n : n + CHUNK] = res.astype(BF16)

            @pl.when(me != last)
            def _():
                send(
                    hout.at[b, :, pl.ds(n, CHUNK)], hist.at[b, :, pl.ds(n, CHUNK)], f_send.at[b], f_recv.at[b], to
                ).start()

        @pl.when((me == last) & (holder != last))
        def _():
            send(hout.at[b], orecv.at[lax.rem(b, per)], f_send.at[b], o_recv.at[lax.rem(b, per)], holder).start()

        return carry

    lax.fori_loop(0, n_block, forward, 0)

    from_kept = order_matrix(frames, BLOCK, True)

    def give(ref, rows):
        ref[...] = jnp.dot(from_kept, rows.reshape(frames, feature), preferred_element_type=F32).astype(BF16)

    @pl.when(me != last)
    def _():
        for i in range(per):
            send(orecv.at[i], orecv.at[i], f_send.at[i], o_recv.at[i], 0).wait_recv()
        give(out_ref, orecv[...])

    def backward(step, carry):
        b = n_block - 1 - step

        @pl.when((me != last) | (b < n_block - per))
        def _():
            send(gin.at[b], gin.at[b], b_send.at[b], b_recv.at[b], 0).wait_recv()

        g = gin[b]
        masked = jnp.where(valid_rows(b), g.astype(F32), 0.0).astype(BF16)
        gp[b] = masked
        for n in range(0, feature, CHUNK):
            ga = jnp.dot(masked, w[:, n : n + CHUNK], preferred_element_type=F32)
            gc[b, :, n : n + CHUNK] = ga * slope[b, :, n : n + CHUNK]

        inverse = [inv[b, 8 * r : 8 * r + 8, 0:1] for r in range(groups)]

        def scaled_of(cols):
            rows = hist[b, :, cols].astype(F32)
            return [rows[8 * r : 8 * r + 8] * inverse[r] for r in range(groups)]

        def column(c, sums):
            cols = cols_of(c)
            now = [gc[b, 8 * r : 8 * r + 8, cols] for r in range(groups)]
            later = [gc[b + 1, 8 * r : 8 * r + 8, cols] for r in range(groups)]
            shifted = {r: now[r] for r in range(groups)}
            for e in range(groups, groups + halo):
                q, r = divmod(e, groups)
                shifted[e] = pltpu.roll(jnp.where(sub < q, later[r], now[r]), 8 - q, 0)
            base = [normed[b + 1, 8 * r : 8 * r + 8, cols] for r in range(groups)]
            total = [None] * groups
            for k in range(taps):
                tap = kb[k, :, cols]
                grown = kacc[k, :, cols]
                for r in range(groups):
                    value = shifted[r + halo - k]
                    term = tap * value
                    total[r] = term if k == 0 else total[r] + term
                    grown = grown + value * base[r]
                kacc[k, :, cols] = grown
            scaled = scaled_of(cols)
            gain = kb[taps, :, cols]
            grown = gacc[:, cols]
            sums = list(sums)
            for r in range(groups):
                product = total[r] * scaled[r]
                grown = grown + product
                gh[8 * r : 8 * r + 8, cols] = total[r] * gain
                product = product * gain
                for p in range(0, COLUMNS, 128):
                    sums[r] = sums[r] + product[:, p : p + 128]
            gacc[:, cols] = grown
            return tuple(sums)

        sums = lax.fori_loop(
            0, feature // COLUMNS, column, tuple(jnp.zeros((8, 128), F32) for _ in range(groups))
        )
        means = jnp.concatenate([jnp.sum(s, axis=1, keepdims=True) for s in sums], axis=0) * (1.0 / feature)
        inverse_all = inv[b, :, 0:1]
        to = jnp.maximum(me - 1, 0)
        holder = lax.div(b, per)
        for n in range(0, feature, CHUNK):
            cols = slice(n, n + CHUNK)
            scaled = hist[b, :, cols].astype(F32) * inverse_all
            grad_h = inverse_all * (gh[:, cols] - scaled * means)
            gout[b, :, cols] = (gin[b, :, cols].astype(F32) + grad_h).astype(BF16)

            @pl.when(me != 0)
            def _():
                send(
                    gout.at[b, :, pl.ds(n, CHUNK)], gin.at[b, :, pl.ds(n, CHUNK)], b_send.at[b], b_recv.at[b], to
                ).start()

        @pl.when((me == 0) & (holder != 0))
        def _():
            send(gout.at[b], irecv.at[lax.rem(b, per)], b_send.at[b], i_recv.at[lax.rem(b, per)], holder).start()

        return carry

    lax.fori_loop(0, n_block, backward, 0)

    @pl.when(me == last)
    def _():
        give(out_ref, hout[n_block - per : n_block])

    @pl.when(me == 0)
    def _():
        give(igrad_ref, gout[0:per])

    rows_own = feature // (4 * RING)
    width = feature // 2
    quarter = feature // 4

    def lanes(start, size):
        return pl.ds(pl.multiple_of(start, 128), size)

    s_own[0:taps, :] = jnp.sum(kacc[...], axis=1).astype(BF16)
    s_own[taps : taps + 1, :] = jnp.sum(gacc[...], axis=0, keepdims=True).astype(BF16)
    s1 = send(s_own.at[:, lanes((1 - core) * width, width)], s_core, s_send.at[0], s_recv.at[0], other_core)
    s1.start()

    batch = 4 * 2 * rows_own

    def core_copy(j):
        return send(
            wgl.at[pl.ds(4 * j, 4), 1 - core], core_in.at[pl.ds(4 * j, 4)], wg_send, wg_recv.at[j], other_core
        )

    def weight_rows(j, carry):
        left = gp[:, :, lanes(j * batch, batch)].reshape(n_block * BLOCK, batch)
        right = act[...].reshape(n_block * BLOCK, feature)
        part = lax.dot_general(left, right, (((0,), (0,)), ((), ())), preferred_element_type=F32)
        wgl[pl.ds(4 * j, 4)] = part.astype(BF16).reshape(4, 2, rows_own, feature)
        core_copy(j).start()
        return carry

    lax.fori_loop(0, 2 * RING // 4, weight_rows, 0)

    s1.wait_recv()
    s_half[...] = (s_own[:, lanes(core * width, width)].astype(F32) + s_core[...].astype(F32)).astype(BF16)
    s2 = send(s_half.at[:, lanes((1 - y) * quarter, quarter)], s_y, s_send.at[1], s_recv.at[1], other_y)
    s2.start()

    for j in range(2 * RING // 4):
        core_copy(j).wait_recv()

    def own(y_at, z_at, half):
        at = y_at * RING + z_at
        cols = slice(half * width, half * width + width)
        return wgl[at, core, :, cols].astype(F32) + core_in[at, :, cols].astype(F32)

    first = {(0, 0): HALF, (0, 1): HALF - 1, (1, 0): HALF - 1, (1, 1): HALF, (2, 0): HALF, (2, 1): HALF - 1}

    def value(which, z_at, slot):
        if which < 2:
            return own(which, z_at, 0)
        return own(y, z_at, 1) + y_in[slot].astype(F32)

    def z_copy(which, way, k):
        at = (which * 2 + way) * HALF
        step = -1 if way == 0 else 1
        return send(
            z_out.at[at + k - 1], z_in.at[at + k - 1], z_send.at[at + k - 1], z_recv.at[at + k - 1],
            peer(y, around(step), core),
        )

    def y_slot(k):
        return k % RING

    def y_copy(k):
        return send(y_out.at[y_slot(k)], y_in.at[y_slot(k)], y_send.at[y_slot(k)], y_recv.at[y_slot(k)], other_y)

    def hop(which, way, k):
        if k > first[which, way]:
            return
        offset = -k if way == 0 else k
        if which == 2:
            y_copy(offset).wait_recv()
        at = (which * 2 + way) * HALF
        total = value(which, around(offset), y_slot(offset))
        if k < first[which, way]:
            z_copy(which, way, k + 1).wait_recv()
            total = total + z_in[at + k].astype(F32)
        z_out[at + k - 1] = total.astype(BF16)
        z_copy(which, way, k).start()

    def y_start(k):
        y_out[y_slot(k)] = own(1 - y, around(k), 1).astype(BF16)
        y_copy(k).start()

    def hops(sets, k):
        for which in sets:
            for way in (0, 1):
                hop(which, way, k)

    hops((0, 1), 4)
    y_start(-4)
    y_start(-3)
    y_start(3)
    hops((0, 1), 3)
    for k in (-2, 2, -1, 1, 0):
        y_start(k)

    s2.wait_recv()
    s_z[z] = (s_half[:, lanes(y * quarter, quarter)].astype(F32) + s_y[...].astype(F32)).astype(BF16)

    def s_copy(k):
        return send(s_z.at[z], s_z.at[z], s_send.at[2], s_recv.at[2], peer(y, around(k), core))

    for k in range(1, RING):
        s_copy(k).start()

    hops((2,), 4)
    hops((0, 1), 2)
    hops((2,), 3)
    hops((0, 1), 1)
    hops((2,), 2)

    def total_of(which, z_at, slot):
        total = value(which, z_at, slot)
        for way in (0, 1):
            z_copy(which, way, 1).wait_recv()
            total = total + z_in[(which * 2 + way) * HALF].astype(F32)
        return total

    for which in (0, 1):
        total = total_of(which, z, 0)

        @pl.when(y == which)
        def _():
            wg_ref[:, 0:width] = total

        @pl.when(y != which)
        def _():
            last_out[...] = total.astype(BF16)

    last_copy = send(last_out, last_in, last_sem.at[0], last_sem.at[1], other_y)
    last_copy.start()
    hops((2,), 1)

    send(s_z.at[pl.ds(0, RING - 1)], s_z.at[pl.ds(0, RING - 1)], s_send.at[2], s_recv.at[2], other_y).wait_recv()
    fin = s_z[0].astype(F32)
    for k in range(1, RING):
        fin = fin + s_z[k].astype(F32)
    s_fin[:, lanes(y * quarter, quarter)] = fin.astype(BF16)
    mine = s_fin.at[:, lanes(y * quarter, quarter)]
    s4 = send(mine, s_fin.at[:, lanes(y * quarter, quarter)], s_send.at[3], s_recv.at[3], other_y)
    s4.start()
    s4.wait_recv()
    s5 = send(s_fin, s_got, s_send.at[4], s_recv.at[4], other_core)
    s5.start()

    y_copy(0).wait_recv()
    wg_ref[:, width:feature] = total_of(2, z, 0)
    last_copy.wait_recv()
    wg_ref[:, 0:width] = wg_ref[:, 0:width] + last_in[...].astype(F32)

    s5.wait_recv()
    s_back[:, lanes(core * width, width)] = s_fin[...].astype(F32)
    s_back[:, lanes((1 - core) * width, width)] = s_got[...].astype(F32)
    kgrad_ref[...] = s_back[0:taps, :]
    ggrad_ref[...] = s_back[taps : taps + 1, :]

    s1.wait_send()
    s2.wait_send()
    send(s_z.at[pl.ds(0, RING - 1)], s_z.at[pl.ds(0, RING - 1)], s_send.at[2], s_recv.at[2], other_y).wait_send()
    s4.wait_send()
    s5.wait_send()
    last_copy.wait_send()
    send(core_in, core_in, wg_send, wg_recv.at[0], other_core).wait_send()
    for k in range(-HALF, HALF):
        y_copy(k).wait_send()
    for (which, way), start in first.items():
        for k in range(1, start + 1):
            z_copy(which, way, k).wait_send()

    @pl.when(me != 0)
    def _():
        for i in range(per):
            send(irecv.at[i], irecv.at[i], b_send.at[i], i_recv.at[i], 0).wait_recv()
        give(igrad_ref, irecv[...])

    @pl.when(me != 0)
    def _():
        send(xin, xin, x_send, o_recv.at[0], 0).wait_send()

    @pl.when(me != last)
    def _():
        send(cin, cin, c_send, o_recv.at[0], 0).wait_send()

    def sent(b, carry):
        @pl.when((me != last) | (b < n_block - per))
        def _():
            send(hout.at[b], hist.at[b], f_send.at[b], f_recv.at[b], 0).wait_send()

        @pl.when((me != 0) | (b >= per))
        def _():
            send(gout.at[b], gin.at[b], b_send.at[b], b_recv.at[b], 0).wait_send()

        return carry

    lax.fori_loop(0, n_block, sent, 0)


def pipeline(x, lengths, cot, weight, kern, gain):
    sections = lax.axis_size("section")
    frames, feature = x.shape
    taps = kern.shape[0]
    n_block = sections * frames // BLOCK
    per = frames // BLOCK
    vmem = pl.BlockSpec(memory_space=pltpu.VMEM)
    rows_own = feature // lax.axis_size("dp")
    blocks = (n_block, BLOCK, feature)
    own = (per, BLOCK, feature)
    return pl.pallas_call(
        functools.partial(kernel, sections, frames, taps, n_block),
        out_shape=(
            jax.ShapeDtypeStruct((frames, feature), BF16),
            jax.ShapeDtypeStruct((frames, feature), BF16),
            jax.ShapeDtypeStruct((rows_own, feature), F32),
            jax.ShapeDtypeStruct((taps, feature), F32),
            jax.ShapeDtypeStruct((1, feature), F32),
        ),
        in_specs=[
            vmem, pl.BlockSpec(memory_space=pltpu.SMEM), vmem, pl.BlockSpec(memory_space=pl.ANY), vmem, vmem,
        ],
        out_specs=(vmem, vmem, vmem, vmem, vmem),
        scratch_shapes=[
            pltpu.VMEM((feature, feature), BF16),
            pltpu.VMEM((feature, feature), BF16),
            pltpu.VMEM(blocks, BF16),
            pltpu.VMEM(blocks, BF16),
            pltpu.VMEM((n_block + 1, BLOCK, feature), F32),
            pltpu.VMEM(blocks, F32),
            pltpu.VMEM(blocks, BF16),
            pltpu.VMEM((n_block, BLOCK, 128), F32),
            pltpu.VMEM(blocks, BF16),
            pltpu.VMEM(blocks, BF16),
            pltpu.VMEM(blocks, BF16),
            pltpu.VMEM((n_block + 1, BLOCK, feature), F32),
            pltpu.VMEM((BLOCK, feature), F32),
            pltpu.VMEM((taps + 1, 8, feature), F32),
            pltpu.VMEM((taps, 8, feature), F32),
            pltpu.VMEM((8, feature), F32),
            pltpu.VMEM(own, BF16),
            pltpu.VMEM(own, BF16),
            pltpu.VMEM(own, BF16),
            pltpu.VMEM(own, BF16),
            pltpu.VMEM((2 * RING, 2, rows_own, feature), BF16),
            pltpu.VMEM((2 * RING, rows_own, feature), BF16),
            pltpu.VMEM((6 * HALF, rows_own, feature // 2), BF16),
            pltpu.VMEM((6 * HALF, rows_own, feature // 2), BF16),
            pltpu.VMEM((RING, rows_own, feature // 2), BF16),
            pltpu.VMEM((RING, rows_own, feature // 2), BF16),
            pltpu.VMEM((rows_own, feature // 2), BF16),
            pltpu.VMEM((rows_own, feature // 2), BF16),
            pltpu.VMEM((taps + 1, feature), BF16),
            pltpu.VMEM((taps + 1, feature // 2), BF16),
            pltpu.VMEM((taps + 1, feature // 2), BF16),
            pltpu.VMEM((taps + 1, feature // 4), BF16),
            pltpu.VMEM((RING, taps + 1, feature // 4), BF16),
            pltpu.VMEM((taps + 1, feature // 2), BF16),
            pltpu.VMEM((taps + 1, feature // 2), BF16),
            pltpu.VMEM((taps + 1, feature), F32),
            pltpu.SemaphoreType.DMA,
            pltpu.SemaphoreType.DMA((n_block,)),
            pltpu.SemaphoreType.DMA((n_block,)),
            pltpu.SemaphoreType.DMA((n_block,)),
            pltpu.SemaphoreType.DMA((n_block,)),
            pltpu.SemaphoreType.DMA,
            pltpu.SemaphoreType.DMA,
            pltpu.SemaphoreType.DMA((per,)),
            pltpu.SemaphoreType.DMA((per,)),
            pltpu.SemaphoreType.DMA,
            pltpu.SemaphoreType.DMA((2 * RING // 4,)),
            pltpu.SemaphoreType.DMA((6 * HALF,)),
            pltpu.SemaphoreType.DMA((6 * HALF,)),
            pltpu.SemaphoreType.DMA((RING,)),
            pltpu.SemaphoreType.DMA((RING,)),
            pltpu.SemaphoreType.DMA((2,)),
            pltpu.SemaphoreType.DMA((5,)),
            pltpu.SemaphoreType.DMA((5,)),
        ],
        compiler_params=pltpu.CompilerParams(
            collective_id=0, has_side_effects=True, vmem_limit_bytes=60 * 1024 * 1024
        ),
        cost_estimate=pl.CostEstimate(
            flops=6 * n_block * BLOCK * feature * feature, bytes_accessed=4 * feature * feature, transcendentals=0
        ),
    )(x, lengths, cot, weight, kern, gain)


def local(inputs, lengths, cotangent, weight, kern, gain):
    out, igrad, wg, kgrad, ggrad = pipeline(inputs[0], lengths, cotangent[0], weight[0], kern[0], gain)
    return (out[None], igrad[None], wg[None], kgrad[None], ggrad)


def solution(mesh):
    return jax.shard_map(
        local,
        mesh=mesh,
        in_specs=(
            P("dp", "section", None),
            P("dp"),
            P("dp", "section", None),
            P("section", None, None),
            P("section", None, None),
            P("section", None),
        ),
        out_specs=(
            P("dp", "section", None),
            P("dp", "section", None),
            P("section", "dp", None),
            P("section", None, None),
            P("section", None),
        ),
        check_vma=False,
    )
```

```python
import functools

import jax
import jax.numpy as jnp
from jax import lax
from jax.experimental import pallas as pl
from jax.experimental.pallas import tpu as pltpu
from jax.sharding import PartitionSpec as P

EPSILON = 1e-05
BLOCK = 16
COLUMNS = 256
F32 = jnp.float32
BF16 = jnp.bfloat16


def order_matrix(frames, block, back):
    groups = block // 8
    row = lax.broadcasted_iota(jnp.int32, (frames, frames), 0)
    col = lax.broadcasted_iota(jnp.int32, (frames, frames), 1)
    kept, time = (col, row) if back else (row, col)
    inside = lax.rem(kept, block)
    frame = kept - inside + groups * lax.rem(inside, 8) + lax.div(inside, 8)
    return (frame == time).astype(BF16)


RING = 8
HALF = 4


def kernel(
    sections, frames, taps, n_block,
    x_ref, len_ref, cot_ref, w_hbm, kern_ref, gain_ref,
    out_ref, igrad_ref, wg_ref, kgrad_ref, ggrad_ref,
    w, wt, hist, hout, normed, slope, act, inv, gin, gout, gp, gc, gh, kb, kacc, gacc, xin, cin, orecv, irecv,
    act_in, gp_in, wgl, z_out, z_in, final, last_out, last_in, s_own, s_core, s_half, s_y, s_z, s_fin, s_got, s_back,
    w_sem, f_recv, f_send, b_recv, b_send, x_send, c_send, o_recv, i_recv,
    act_send, act_recv, gp_send, gp_recv, z_send, z_recv, last_sem, s_send, s_recv,
):
    me = lax.axis_index("section")
    last = sections - 1
    feature = x_ref.shape[1]
    per = frames // BLOCK
    groups = BLOCK // 8
    halo = taps - 1

    w_copy = pltpu.make_async_copy(w_hbm, w, w_sem)
    w_copy.start()

    dp = lax.axis_index("dp")
    core = lax.rem(dp, 2)
    z = lax.rem(lax.div(dp, 2), RING)
    y = lax.div(dp, 2 * RING)

    def around(offset):
        return lax.rem(z + offset + RING, RING)

    def peer(y_at, z_at, core_at):
        return {"dp": (y_at * RING + z_at) * 2 + core_at}

    other_core = peer(y, z, 1 - core)
    other_y = peer(1 - y, z, core)
    cross = peer(1 - y, z, 1 - core)

    barrier = pltpu.get_barrier_semaphore()
    partners = [{"section": lax.rem(me + d, sections)} for d in range(1, sections)]
    partners += [peer(y, around(d), core) for d in range(1, RING)] + [other_core, other_y, cross]
    for partner in partners:
        pl.semaphore_signal(barrier, inc=1, device_id=partner, device_id_type=pl.DeviceIdType.MESH)

    to_kept = order_matrix(frames, BLOCK, False)
    xin[...] = jnp.dot(to_kept, x_ref[...], preferred_element_type=F32).astype(BF16).reshape(xin.shape)
    cin[...] = jnp.dot(to_kept, cot_ref[...], preferred_element_type=F32).astype(BF16).reshape(cin.shape)

    for k in range(taps):
        kb[k] = jnp.broadcast_to(kern_ref[k], (8, feature))
    normed[0] = jnp.zeros_like(normed[0])
    gc[n_block] = jnp.zeros_like(gc[n_block])
    kacc[...] = jnp.zeros_like(kacc)
    gacc[...] = jnp.zeros_like(gacc)

    @pl.when(me == 0)
    def _():
        for i in range(per):
            hist[i] = xin[i]

    @pl.when(me == last)
    def _():
        for i in range(per):
            gin[n_block - per + i] = cin[i]

    w_copy.wait()

    def turn(i, carry):
        strip = pl.ds(pl.multiple_of(i * COLUMNS, COLUMNS), COLUMNS)
        wt[:, strip] = w[strip, :].T
        return carry

    lax.fori_loop(0, feature // COLUMNS, turn, 0)
    pl.semaphore_wait(barrier, len(partners))

    def send(src, dst, send_sem, recv_sem, to):
        return pltpu.make_async_remote_copy(
            src_ref=src, dst_ref=dst, send_sem=send_sem, recv_sem=recv_sem,
            device_id=to if isinstance(to, dict) else {"section": to}, device_id_type=pl.DeviceIdType.MESH,
        )

    def x_copy(i):
        return send(xin.at[i], hist.at[me * per + i], x_send, f_recv.at[me * per + i], 0)

    def c_copy(i):
        return send(cin.at[i], gin.at[me * per + i], c_send, b_recv.at[me * per + i], last)

    @pl.when(me != 0)
    def _():
        for i in range(per):
            x_copy(i).start()

    @pl.when(me != last)
    def _():
        for i in reversed(range(per)):
            c_copy(i).start()

    width = feature // 2
    quarter = feature // 4

    def lanes(start, size):
        return pl.ds(pl.multiple_of(start, 128), size)

    def share_act(b, slot, to, half):
        send(act.at[b, :, lanes(half * width, width)], act_in.at[slot, b], act_send, act_recv.at[slot], to).start()

    def share_gp(b, slot, to, half):
        send(gp.at[b, :, lanes(half * width, width)], gp_in.at[slot, b], gp_send, gp_recv.at[slot], to).start()

    sub = lax.broadcasted_iota(jnp.int32, (8, COLUMNS), 0)
    length = len_ref[0]

    def valid_rows(b):
        row = lax.broadcasted_iota(jnp.int32, (BLOCK, 1), 0)
        frame = b * BLOCK + groups * lax.rem(row, 8) + lax.div(row, 8)
        return frame < length

    column_slices = [slice(c, c + COLUMNS) for c in range(0, feature, COLUMNS)]

    def forward(b, carry):
        @pl.when((me != 0) | (b >= per))
        def _():
            send(hist.at[b], hist.at[b], f_send.at[b], f_recv.at[b], 0).wait_recv()

        wide = hist[b].astype(F32)
        inverse = lax.rsqrt(jnp.sum(wide * wide, axis=1, keepdims=True) * (1.0 / feature) + EPSILON)
        inv[b] = jnp.broadcast_to(inverse, (BLOCK, 128))
        projected = None
        for cols in column_slices:
            fresh = (wide[:, cols] * inverse) * gain_ref[:, cols]
            normed[b + 1, :, cols] = fresh
            now = [fresh[8 * r : 8 * r + 8] for r in range(groups)]
            past = [normed[b, 8 * r : 8 * r + 8, cols] for r in range(groups)]
            shifted = {r: now[r] for r in range(groups)}
            for m in range(1, halo + 1):
                q = -(-m // groups)
                r = q * groups - m
                shifted[-m] = pltpu.roll(jnp.where(sub >= 8 - q, past[r], now[r]), q, 0)
            total = [None] * groups
            for k in range(taps):
                tap = kb[k, :, cols]
                for r in range(groups):
                    term = tap * shifted[r - halo + k]
                    total[r] = term if k == 0 else total[r] + term
            mixed = jnp.concatenate(total, axis=0)
            sigma = 0.5 * jnp.tanh(0.5 * mixed) + 0.5
            product = mixed * sigma
            slope[b, :, cols] = sigma + product * (1.0 - sigma)
            activated = product.astype(BF16)
            act[b, :, cols] = activated
            part = jnp.dot(activated, wt[cols, :], preferred_element_type=F32)
            projected = part if projected is None else projected + part
        hout[b] = (wide + jnp.where(valid_rows(b), projected, 0.0)).astype(BF16)

        to = jnp.minimum(me + 1, last)
        holder = lax.div(b, per)

        @pl.when(me != last)
        def _():
            send(hout.at[b], hist.at[b], f_send.at[b], f_recv.at[b], to).start()

        @pl.when((me == last) & (holder != last))
        def _():
            send(hout.at[b], orecv.at[lax.rem(b, per)], f_send.at[b], o_recv.at[lax.rem(b, per)], holder).start()

        share_act(b, 0, other_core, 1 - core)
        share_act(b, 1, other_y, core)
        share_act(b, 2, cross, 1 - core)
        return carry

    lax.fori_loop(0, n_block, forward, 0)

    from_kept = order_matrix(frames, BLOCK, True)

    def give(ref, rows):
        ref[...] = jnp.dot(from_kept, rows.reshape(frames, feature), preferred_element_type=F32).astype(BF16)

    @pl.when(me != last)
    def _():
        for i in range(per):
            send(orecv.at[i], orecv.at[i], f_send.at[i], o_recv.at[i], 0).wait_recv()
        give(out_ref, orecv[...])

    def backward(step, carry):
        b = n_block - 1 - step

        @pl.when((me != last) | (b < n_block - per))
        def _():
            send(gin.at[b], gin.at[b], b_send.at[b], b_recv.at[b], 0).wait_recv()

        grad = gin[b].astype(F32)
        masked = jnp.where(valid_rows(b), grad, 0.0).astype(BF16)
        gp[b] = masked
        inverse = inv[b, :, 0:1]
        sums = jnp.zeros((BLOCK, 128), F32)
        for cols in column_slices:
            fresh = jnp.dot(masked, w[:, cols], preferred_element_type=F32) * slope[b, :, cols]
            gc[b, :, cols] = fresh
            now = [fresh[8 * r : 8 * r + 8] for r in range(groups)]
            later = [gc[b + 1, 8 * r : 8 * r + 8, cols] for r in range(groups)]
            shifted = {r: now[r] for r in range(groups)}
            for e in range(groups, groups + halo):
                q, r = divmod(e, groups)
                shifted[e] = pltpu.roll(jnp.where(sub < q, later[r], now[r]), 8 - q, 0)
            base = [normed[b + 1, 8 * r : 8 * r + 8, cols] for r in range(groups)]
            total = [None] * groups
            for k in range(taps):
                tap = kb[k, :, cols]
                grown = kacc[k, :, cols]
                for r in range(groups):
                    value = shifted[r + halo - k]
                    term = tap * value
                    total[r] = term if k == 0 else total[r] + term
                    grown = grown + value * base[r]
                kacc[k, :, cols] = grown
            grad_n = jnp.concatenate(total, axis=0)
            scaled = hist[b, :, cols].astype(F32) * inverse
            product = grad_n * scaled
            for r in range(groups):
                gacc[:, cols] += product[8 * r : 8 * r + 8]
            gh[:, cols] = grad_n * gain_ref[:, cols]
            product = product * gain_ref[:, cols]
            for p in range(0, COLUMNS, 128):
                sums = sums + product[:, p : p + 128]

        mean = jnp.sum(sums, axis=1, keepdims=True) * (1.0 / feature)
        scaled = hist[b].astype(F32) * inverse
        gout[b] = (gin[b].astype(F32) + inverse * (gh[...] - scaled * mean)).astype(BF16)

        to = jnp.maximum(me - 1, 0)
        holder = lax.div(b, per)

        @pl.when(me != 0)
        def _():
            send(gout.at[b], gin.at[b], b_send.at[b], b_recv.at[b], to).start()

        @pl.when((me == 0) & (holder != 0))
        def _():
            send(gout.at[b], irecv.at[lax.rem(b, per)], b_send.at[b], i_recv.at[lax.rem(b, per)], holder).start()

        share_gp(b, 0, other_core, y)
        share_gp(b, 1, other_y, 1 - y)
        share_gp(b, 2, cross, 1 - y)
        return carry

    lax.fori_loop(0, n_block, backward, 0)

    rows_own = feature // (4 * RING)
    total_frames = n_block * BLOCK
    batch = width // 2

    s_own[0:taps, :] = jnp.sum(kacc[...], axis=1).astype(BF16)
    s_own[taps : taps + 1, :] = jnp.sum(gacc[...], axis=0, keepdims=True).astype(BF16)
    s1 = send(s_own.at[:, lanes((1 - core) * width, width)], s_core, s_send.at[0], s_recv.at[0], other_core)
    s1.start()

    def shared(slot):
        send(act_in.at[slot], act_in.at[slot], act_send, act_recv.at[slot], other_core).wait_recv()
        send(gp_in.at[slot], gp_in.at[slot], gp_send, gp_recv.at[slot], other_core).wait_recv()

    def weight_rows(j, wait):
        def product(left, right):
            return lax.dot_general(
                left.reshape(total_frames, batch), right.reshape(total_frames, width),
                (((0,), (0,)), ((), ())), preferred_element_type=F32,
            )

        part = product(gp[:, :, lanes(y * width + j * batch, batch)], act[:, :, lanes(core * width, width)])
        for slot in range(3):
            if wait:
                shared(slot)
            part = part + product(gp_in[slot, :, :, lanes(j * batch, batch)], act_in[slot])
        wgl[pl.ds(j * (RING // 2), RING // 2)] = part.reshape(RING // 2, 2 * rows_own, width)

    first = {(0, 0): HALF, (0, 1): HALF - 1, (1, 0): HALF - 1, (1, 1): HALF}

    def columns_of(which):
        return slice(which * quarter, (which + 1) * quarter)

    def z_copy(which, way, k):
        at = (which * 2 + way) * HALF + k - 1
        step = -1 if way == 0 else 1
        return send(z_out.at[at], z_in.at[at], z_send.at[at], z_recv.at[at], peer(y, around(step), core))

    def hop(which, way, k):
        at = (which * 2 + way) * HALF + k - 1
        total = wgl[around(-k if way == 0 else k), :, columns_of(which)]
        if k < first[which, way]:
            z_copy(which, way, k + 1).wait_recv()
            total = total + z_in[at + 1].astype(F32)
        z_out[at] = total.astype(BF16)
        z_copy(which, way, k).start()

    early = lax.div(around(HALF), RING // 2)
    weight_rows(early, True)
    hop(0, 0, 4)
    hop(1, 1, 4)

    s1.wait_recv()
    s_half[...] = (s_own[:, lanes(core * width, width)].astype(F32) + s_core[...].astype(F32)).astype(BF16)
    s2 = send(s_half.at[:, lanes((1 - y) * quarter, quarter)], s_y, s_send.at[1], s_recv.at[1], other_y)
    s2.start()

    weight_rows(1 - early, False)
    hop(0, 1, 3)
    hop(1, 0, 3)
    hop(0, 0, 3)
    hop(1, 1, 3)

    s2.wait_recv()
    s_z[z] = (s_half[:, lanes(y * quarter, quarter)].astype(F32) + s_y[...].astype(F32)).astype(BF16)

    def s_copy(k):
        return send(s_z.at[z], s_z.at[z], s_send.at[2], s_recv.at[2], peer(y, around(k), core))

    for k in range(1, RING):
        s_copy(k).start()

    for k in (2, 1):
        hop(0, 1, k)
        hop(1, 0, k)
        hop(0, 0, k)
        hop(1, 1, k)

    send(s_z.at[pl.ds(0, RING - 1)], s_z.at[pl.ds(0, RING - 1)], s_send.at[2], s_recv.at[2], other_y).wait_recv()
    fin = s_z[0].astype(F32)
    for k in range(1, RING):
        fin = fin + s_z[k].astype(F32)
    s_fin[:, lanes(y * quarter, quarter)] = fin.astype(BF16)
    mine = s_fin.at[:, lanes(y * quarter, quarter)]
    s4 = send(mine, s_fin.at[:, lanes(y * quarter, quarter)], s_send.at[3], s_recv.at[3], other_y)
    s4.start()

    for which in (0, 1):
        total = wgl[z, :, columns_of(which)]
        for way in (0, 1):
            z_copy(which, way, 1).wait_recv()
            total = total + z_in[(which * 2 + way) * HALF].astype(F32)
        final[:, :, columns_of(which)] = total.reshape(2, rows_own, quarter)
    last_out[...] = final[1 - core].astype(BF16)
    last_copy = send(last_out, last_in, last_sem.at[0], last_sem.at[1], other_core)
    last_copy.start()
    wg_ref[:, lanes(core * width, width)] = final[core]

    s4.wait_recv()
    s5 = send(s_fin, s_got, s_send.at[4], s_recv.at[4], other_core)
    s5.start()
    last_copy.wait_recv()
    wg_ref[:, lanes((1 - core) * width, width)] = last_in[...].astype(F32)

    s5.wait_recv()
    s_back[:, lanes(core * width, width)] = s_fin[...].astype(F32)
    s_back[:, lanes((1 - core) * width, width)] = s_got[...].astype(F32)
    for k in range(taps):
        kgrad_ref[k] = s_back[k : k + 1, :]
    ggrad_ref[...] = s_back[taps : taps + 1, :]

    s1.wait_send()
    s2.wait_send()
    send(s_z.at[pl.ds(0, RING - 1)], s_z.at[pl.ds(0, RING - 1)], s_send.at[2], s_recv.at[2], other_y).wait_send()
    s4.wait_send()
    s5.wait_send()
    last_copy.wait_send()
    send(act_in, act_in, act_send, act_recv.at[0], other_core).wait_send()
    send(gp_in, gp_in, gp_send, gp_recv.at[0], other_core).wait_send()
    for (which, way), start in first.items():
        for k in range(1, start + 1):
            z_copy(which, way, k).wait_send()

    @pl.when(me == last)
    def _():
        give(out_ref, hout[n_block - per : n_block])

    @pl.when(me == 0)
    def _():
        give(igrad_ref, gout[0:per])

    @pl.when(me != 0)
    def _():
        for i in range(per):
            send(irecv.at[i], irecv.at[i], b_send.at[i], i_recv.at[i], 0).wait_recv()
        give(igrad_ref, irecv[...])

    @pl.when(me != 0)
    def _():
        send(xin, xin, x_send, o_recv.at[0], 0).wait_send()

    @pl.when(me != last)
    def _():
        send(cin, cin, c_send, o_recv.at[0], 0).wait_send()

    def sent(b, carry):
        @pl.when((me != last) | (b < n_block - per))
        def _():
            send(hout.at[b], hist.at[b], f_send.at[b], f_recv.at[b], 0).wait_send()

        @pl.when((me != 0) | (b >= per))
        def _():
            send(gout.at[b], gin.at[b], b_send.at[b], b_recv.at[b], 0).wait_send()

        return carry

    lax.fori_loop(0, n_block, sent, 0)


def pipeline(x, lengths, cot, weight, kern, gain):
    sections = lax.axis_size("section")
    frames, feature = x.shape
    taps = kern.shape[0]
    n_block = sections * frames // BLOCK
    per = frames // BLOCK
    vmem = pl.BlockSpec(memory_space=pltpu.VMEM)
    rows_own = feature // lax.axis_size("dp")
    blocks = (n_block, BLOCK, feature)
    own = (per, BLOCK, feature)
    return pl.pallas_call(
        functools.partial(kernel, sections, frames, taps, n_block),
        out_shape=(
            jax.ShapeDtypeStruct((frames, feature), BF16),
            jax.ShapeDtypeStruct((frames, feature), BF16),
            jax.ShapeDtypeStruct((rows_own, feature), F32),
            jax.ShapeDtypeStruct((taps, 1, feature), F32),
            jax.ShapeDtypeStruct((1, feature), F32),
        ),
        in_specs=[
            vmem, pl.BlockSpec(memory_space=pltpu.SMEM), vmem, pl.BlockSpec(memory_space=pl.ANY), vmem, vmem,
        ],
        out_specs=(vmem, vmem, vmem, vmem, vmem),
        scratch_shapes=[
            pltpu.VMEM((feature, feature), BF16),
            pltpu.VMEM((feature, feature), BF16),
            pltpu.VMEM(blocks, BF16),
            pltpu.VMEM(blocks, BF16),
            pltpu.VMEM((n_block + 1, BLOCK, feature), F32),
            pltpu.VMEM(blocks, F32),
            pltpu.VMEM(blocks, BF16),
            pltpu.VMEM((n_block, BLOCK, 128), F32),
            pltpu.VMEM(blocks, BF16),
            pltpu.VMEM(blocks, BF16),
            pltpu.VMEM(blocks, BF16),
            pltpu.VMEM((n_block + 1, BLOCK, feature), F32),
            pltpu.VMEM((BLOCK, feature), F32),
            pltpu.VMEM((taps, 8, feature), F32),
            pltpu.VMEM((taps, 8, feature), F32),
            pltpu.VMEM((8, feature), F32),
            pltpu.VMEM(own, BF16),
            pltpu.VMEM(own, BF16),
            pltpu.VMEM(own, BF16),
            pltpu.VMEM(own, BF16),
            pltpu.VMEM((3, n_block, BLOCK, feature // 2), BF16),
            pltpu.VMEM((3, n_block, BLOCK, feature // 2), BF16),
            pltpu.VMEM((RING, 2 * rows_own, feature // 2), F32),
            pltpu.VMEM((4 * HALF, 2 * rows_own, feature // 4), BF16),
            pltpu.VMEM((4 * HALF, 2 * rows_own, feature // 4), BF16),
            pltpu.VMEM((2, rows_own, feature // 2), F32),
            pltpu.VMEM((rows_own, feature // 2), BF16),
            pltpu.VMEM((rows_own, feature // 2), BF16),
            pltpu.VMEM((taps + 1, feature), BF16),
            pltpu.VMEM((taps + 1, feature // 2), BF16),
            pltpu.VMEM((taps + 1, feature // 2), BF16),
            pltpu.VMEM((taps + 1, feature // 4), BF16),
            pltpu.VMEM((RING, taps + 1, feature // 4), BF16),
            pltpu.VMEM((taps + 1, feature // 2), BF16),
            pltpu.VMEM((taps + 1, feature // 2), BF16),
            pltpu.VMEM((taps + 1, feature), F32),
            pltpu.SemaphoreType.DMA,
            pltpu.SemaphoreType.DMA((n_block,)),
            pltpu.SemaphoreType.DMA((n_block,)),
            pltpu.SemaphoreType.DMA((n_block,)),
            pltpu.SemaphoreType.DMA((n_block,)),
            pltpu.SemaphoreType.DMA,
            pltpu.SemaphoreType.DMA,
            pltpu.SemaphoreType.DMA((per,)),
            pltpu.SemaphoreType.DMA((per,)),
            pltpu.SemaphoreType.DMA,
            pltpu.SemaphoreType.DMA((3,)),
            pltpu.SemaphoreType.DMA,
            pltpu.SemaphoreType.DMA((3,)),
            pltpu.SemaphoreType.DMA((4 * HALF,)),
            pltpu.SemaphoreType.DMA((4 * HALF,)),
            pltpu.SemaphoreType.DMA((2,)),
            pltpu.SemaphoreType.DMA((5,)),
            pltpu.SemaphoreType.DMA((5,)),
        ],
        compiler_params=pltpu.CompilerParams(
            collective_id=0, has_side_effects=True, vmem_limit_bytes=60 * 1024 * 1024
        ),
        cost_estimate=pl.CostEstimate(
            flops=6 * n_block * BLOCK * feature * feature, bytes_accessed=4 * feature * feature, transcendentals=0
        ),
    )(x, lengths, cot, weight, kern, gain)


def hand_over(*refs):
    count = len(refs) // 2
    for taken, given in zip(refs[:count], refs[count:]):
        given[...] = taken[...]


def local(inputs, lengths, cotangent, weight, kern, gain):
    results = pipeline(inputs[0], lengths, cotangent[0], weight[0], jnp.transpose(kern, (1, 0, 2)), gain)
    vmem = pl.BlockSpec(memory_space=pltpu.VMEM)
    out, igrad, wg, kgrad, ggrad = pl.pallas_call(
        hand_over,
        out_shape=tuple(jax.ShapeDtypeStruct(r.shape, r.dtype) for r in results),
        in_specs=[vmem] * len(results),
        out_specs=(vmem,) * len(results),
    )(*results)
    return (out[None], igrad[None], wg[None], jnp.transpose(kgrad, (1, 0, 2)), ggrad)


def solution(mesh):
    return jax.shard_map(
        local,
        mesh=mesh,
        in_specs=(
            P("dp", "section", None),
            P("dp"),
            P("dp", "section", None),
            P("section", None, None),
            P("section", None, None),
            P("section", None),
        ),
        out_specs=(
            P("dp", "section", None),
            P("dp", "section", None),
            P("section", "dp", None),
            P("section", None, None),
            P("section", None),
        ),
        check_vma=False,
    )
```

```python
import functools

import jax
import jax.numpy as jnp
from jax import lax
from jax.experimental import pallas as pl
from jax.experimental.pallas import tpu as pltpu
from jax.sharding import PartitionSpec as P

EPSILON = 1e-05
BLOCK = 16
COLUMNS = 256
F32 = jnp.float32
BF16 = jnp.bfloat16


def order_matrix(frames, block, back):
    groups = block // 8
    row = lax.broadcasted_iota(jnp.int32, (frames, frames), 0)
    col = lax.broadcasted_iota(jnp.int32, (frames, frames), 1)
    kept, time = (col, row) if back else (row, col)
    inside = lax.rem(kept, block)
    frame = kept - inside + groups * lax.rem(inside, 8) + lax.div(inside, 8)
    return (frame == time).astype(BF16)


RING = 8
HALF = 4


def kernel(
    sections, frames, taps, n_block,
    x_hbm, len_ref, cot_hbm, w_hbm, kern_hbm, gain_hbm,
    out_ref, igrad_ref, wg_ref, kgrad_ref, ggrad_ref,
    x_ref, cot_ref, kern_ref, gain_ref, w, wt, hist, hout, normed, slope, act, inv, gin, gout, gp, gc, gh, kb, kacc, gacc, xin, cin, orecv, irecv,
    act_in, gp_in, wgl, z_out, z_in, final, last_out, last_in, s_own, s_core, s_half, s_y, s_z, s_fin, s_got, s_back,
    w_sem, arg_sems, f_recv, f_send, b_recv, b_send, x_send, c_send, o_recv, i_recv,
    act_send, act_recv, gp_send, gp_recv, z_send, z_recv, last_sem, s_send, s_recv,
):
    me = lax.axis_index("section")
    last = sections - 1
    feature = x_ref.shape[1]
    per = frames // BLOCK
    groups = BLOCK // 8
    halo = taps - 1

    dp = lax.axis_index("dp")
    core = lax.rem(dp, 2)
    z = lax.rem(lax.div(dp, 2), RING)
    y = lax.div(dp, 2 * RING)

    def around(offset):
        return lax.rem(z + offset + RING, RING)

    def peer(y_at, z_at, core_at):
        return {"dp": (y_at * RING + z_at) * 2 + core_at}

    other_core = peer(y, z, 1 - core)
    other_y = peer(1 - y, z, core)
    cross = peer(1 - y, z, 1 - core)

    barrier = pltpu.get_barrier_semaphore()
    partners = [{"section": lax.rem(me + d, sections)} for d in range(1, sections)]
    partners += [peer(y, around(d), core) for d in range(1, RING)] + [other_core, other_y, cross]
    for partner in partners:
        pl.semaphore_signal(barrier, inc=1, device_id=partner, device_id_type=pl.DeviceIdType.MESH)

    w_copy = pltpu.make_async_copy(w_hbm, w, w_sem)
    arg_copies = [
        pltpu.make_async_copy(source, ref, arg_sems.at[i])
        for i, (source, ref) in enumerate(
            [(x_hbm, x_ref), (cot_hbm, cot_ref), (kern_hbm, kern_ref), (gain_hbm, gain_ref)]
        )
    ]
    for copy in arg_copies:
        copy.start()
    w_copy.start()
    for copy in arg_copies:
        copy.wait()

    to_kept = order_matrix(frames, BLOCK, False)
    xin[...] = jnp.dot(to_kept, x_ref[...], preferred_element_type=F32).astype(BF16).reshape(xin.shape)
    cin[...] = jnp.dot(to_kept, cot_ref[...], preferred_element_type=F32).astype(BF16).reshape(cin.shape)

    for k in range(taps):
        kb[k] = jnp.broadcast_to(kern_ref[k], (8, feature))
    normed[0] = jnp.zeros_like(normed[0])
    gc[n_block] = jnp.zeros_like(gc[n_block])
    kacc[...] = jnp.zeros_like(kacc)
    gacc[...] = jnp.zeros_like(gacc)

    @pl.when(me == 0)
    def _():
        for i in range(per):
            hist[i] = xin[i]

    @pl.when(me == last)
    def _():
        for i in range(per):
            gin[n_block - per + i] = cin[i]

    w_copy.wait()

    def turn(i, carry):
        strip = pl.ds(pl.multiple_of(i * COLUMNS, COLUMNS), COLUMNS)
        wt[:, strip] = w[strip, :].T
        return carry

    lax.fori_loop(0, feature // COLUMNS, turn, 0)
    pl.semaphore_wait(barrier, len(partners))

    def send(src, dst, send_sem, recv_sem, to):
        return pltpu.make_async_remote_copy(
            src_ref=src, dst_ref=dst, send_sem=send_sem, recv_sem=recv_sem,
            device_id=to if isinstance(to, dict) else {"section": to}, device_id_type=pl.DeviceIdType.MESH,
        )

    def x_copy(i):
        return send(xin.at[i], hist.at[me * per + i], x_send, f_recv.at[me * per + i], 0)

    def c_copy(i):
        return send(cin.at[i], gin.at[me * per + i], c_send, b_recv.at[me * per + i], last)

    @pl.when(me != 0)
    def _():
        for i in range(per):
            x_copy(i).start()

    @pl.when(me != last)
    def _():
        for i in reversed(range(per)):
            c_copy(i).start()

    width = feature // 2
    quarter = feature // 4

    def lanes(start, size):
        return pl.ds(pl.multiple_of(start, 128), size)

    def share_act(b, slot, to, half):
        send(act.at[b, :, lanes(half * width, width)], act_in.at[slot, b], act_send, act_recv.at[slot], to).start()

    def share_gp(b):
        for slot, to, half in ((2, cross, 1 - y), (1, other_y, 1 - y), (0, other_core, y)):
            send(gp.at[b, :, lanes(half * width, width)], gp_in.at[slot, b], gp_send, gp_recv.at[slot], to).start()

    sub = lax.broadcasted_iota(jnp.int32, (8, COLUMNS), 0)
    length = len_ref[0]

    def valid_rows(b):
        row = lax.broadcasted_iota(jnp.int32, (BLOCK, 1), 0)
        frame = b * BLOCK + groups * lax.rem(row, 8) + lax.div(row, 8)
        return frame < length

    column_slices = [slice(c, c + COLUMNS) for c in range(0, feature, COLUMNS)]

    def forward(b, carry):
        @pl.when((me != 0) | (b >= per))
        def _():
            send(hist.at[b], hist.at[b], f_send.at[b], f_recv.at[b], 0).wait_recv()

        wide = hist[b].astype(F32)
        inverse = lax.rsqrt(jnp.sum(wide * wide, axis=1, keepdims=True) * (1.0 / feature) + EPSILON)
        inv[b] = jnp.broadcast_to(inverse, (BLOCK, 128))
        projected = None
        for cols in column_slices:
            fresh = (wide[:, cols] * inverse) * gain_ref[:, cols]
            normed[b + 1, :, cols] = fresh
            now = [fresh[8 * r : 8 * r + 8] for r in range(groups)]
            past = [normed[b, 8 * r : 8 * r + 8, cols] for r in range(groups)]
            shifted = {r: now[r] for r in range(groups)}
            for m in range(1, halo + 1):
                q = -(-m // groups)
                r = q * groups - m
                shifted[-m] = pltpu.roll(jnp.where(sub >= 8 - q, past[r], now[r]), q, 0)
            total = [None] * groups
            for k in range(taps):
                tap = kb[k, :, cols]
                for r in range(groups):
                    term = tap * shifted[r - halo + k]
                    total[r] = term if k == 0 else total[r] + term
            mixed = jnp.concatenate(total, axis=0)
            sigma = 0.5 * jnp.tanh(0.5 * mixed) + 0.5
            product = mixed * sigma
            slope[b, :, cols] = sigma + product * (1.0 - sigma)
            activated = product.astype(BF16)
            act[b, :, cols] = activated
            part = jnp.dot(activated, wt[cols, :], preferred_element_type=F32)
            projected = part if projected is None else projected + part
        hout[b] = (wide + jnp.where(valid_rows(b), projected, 0.0)).astype(BF16)

        to = jnp.minimum(me + 1, last)
        holder = lax.div(b, per)

        @pl.when(me != last)
        def _():
            send(hout.at[b], hist.at[b], f_send.at[b], f_recv.at[b], to).start()

        @pl.when((me == last) & (holder != last))
        def _():
            send(hout.at[b], orecv.at[lax.rem(b, per)], f_send.at[b], o_recv.at[lax.rem(b, per)], holder).start()

        share_act(b, 0, other_core, 1 - core)
        share_act(b, 1, other_y, core)
        share_act(b, 2, cross, 1 - core)
        return carry

    lax.fori_loop(0, n_block, forward, 0)

    from_kept = order_matrix(frames, BLOCK, True)

    def give(ref, rows):
        ref[...] = jnp.dot(from_kept, rows.reshape(frames, feature), preferred_element_type=F32).astype(BF16)

    @pl.when(me != last)
    def _():
        for i in range(per):
            send(orecv.at[i], orecv.at[i], f_send.at[i], o_recv.at[i], 0).wait_recv()
        give(out_ref, orecv[...])

    def backward(step, carry):
        b = n_block - 1 - step

        @pl.when((me != last) | (b < n_block - per))
        def _():
            send(gin.at[b], gin.at[b], b_send.at[b], b_recv.at[b], 0).wait_recv()

        grad = gin[b].astype(F32)
        masked = jnp.where(valid_rows(b), grad, 0.0).astype(BF16)
        gp[b] = masked

        @pl.when(b == 0)
        def _():
            share_gp(b)

        inverse = inv[b, :, 0:1]
        sums = jnp.zeros((BLOCK, 128), F32)
        for cols in column_slices:
            fresh = jnp.dot(masked, w[:, cols], preferred_element_type=F32) * slope[b, :, cols]
            gc[b, :, cols] = fresh
            now = [fresh[8 * r : 8 * r + 8] for r in range(groups)]
            later = [gc[b + 1, 8 * r : 8 * r + 8, cols] for r in range(groups)]
            shifted = {r: now[r] for r in range(groups)}
            for e in range(groups, groups + halo):
                q, r = divmod(e, groups)
                shifted[e] = pltpu.roll(jnp.where(sub < q, later[r], now[r]), 8 - q, 0)
            base = [normed[b + 1, 8 * r : 8 * r + 8, cols] for r in range(groups)]
            total = [None] * groups
            for k in range(taps):
                tap = kb[k, :, cols]
                grown = kacc[k, :, cols]
                for r in range(groups):
                    value = shifted[r + halo - k]
                    term = tap * value
                    total[r] = term if k == 0 else total[r] + term
                    grown = grown + value * base[r]
                kacc[k, :, cols] = grown
            grad_n = jnp.concatenate(total, axis=0)
            scaled = hist[b, :, cols].astype(F32) * inverse
            product = grad_n * scaled
            for r in range(groups):
                gacc[:, cols] += product[8 * r : 8 * r + 8]
            gh[:, cols] = grad_n * gain_ref[:, cols]
            product = product * gain_ref[:, cols]
            for p in range(0, COLUMNS, 128):
                sums = sums + product[:, p : p + 128]

        mean = jnp.sum(sums, axis=1, keepdims=True) * (1.0 / feature)
        scaled = hist[b].astype(F32) * inverse
        gout[b] = (gin[b].astype(F32) + inverse * (gh[...] - scaled * mean)).astype(BF16)

        to = jnp.maximum(me - 1, 0)
        holder = lax.div(b, per)

        @pl.when(me != 0)
        def _():
            send(gout.at[b], gin.at[b], b_send.at[b], b_recv.at[b], to).start()

        @pl.when((me == 0) & (holder != 0))
        def _():
            send(gout.at[b], irecv.at[lax.rem(b, per)], b_send.at[b], i_recv.at[lax.rem(b, per)], holder).start()

        @pl.when(b != 0)
        def _():
            share_gp(b)

        return carry

    lax.fori_loop(0, n_block, backward, 0)

    rows_own = feature // (4 * RING)
    total_frames = n_block * BLOCK
    batch = width // 2

    s_own[0:taps, :] = jnp.sum(kacc[...], axis=1).astype(BF16)
    s_own[taps : taps + 1, :] = jnp.sum(gacc[...], axis=0, keepdims=True).astype(BF16)
    s1 = send(s_own.at[:, lanes((1 - core) * width, width)], s_core, s_send.at[0], s_recv.at[0], other_core)
    s1.start()

    def shared(slot):
        send(act_in.at[slot], act_in.at[slot], act_send, act_recv.at[slot], other_core).wait_recv()
        send(gp_in.at[slot], gp_in.at[slot], gp_send, gp_recv.at[slot], other_core).wait_recv()

    def product(left, right):
        return lax.dot_general(
            left.reshape(total_frames, batch), right.reshape(total_frames, width),
            (((0,), (0,)), ((), ())), preferred_element_type=F32,
        )

    def rows_of(j):
        return pl.ds(j * (RING // 2), RING // 2)

    def near_rows(j):
        part = product(gp[:, :, lanes(y * width + j * batch, batch)], act[:, :, lanes(core * width, width)])
        part = part + product(gp_in[0, :, :, lanes(j * batch, batch)], act_in[0])
        wgl[rows_of(j)] = part.reshape(RING // 2, 2 * rows_own, width)

    def far_rows(j):
        part = product(gp_in[1, :, :, lanes(j * batch, batch)], act_in[1])
        part = part + product(gp_in[2, :, :, lanes(j * batch, batch)], act_in[2])
        wgl[rows_of(j)] += part.reshape(RING // 2, 2 * rows_own, width)

    first = {(0, 0): HALF, (0, 1): HALF - 1, (1, 0): HALF - 1, (1, 1): HALF}

    def columns_of(which):
        return slice(which * quarter, (which + 1) * quarter)

    def z_copy(which, way, k):
        at = (which * 2 + way) * HALF + k - 1
        step = -1 if way == 0 else 1
        return send(z_out.at[at], z_in.at[at], z_send.at[at], z_recv.at[at], peer(y, around(step), core))

    def hop(which, way, k):
        at = (which * 2 + way) * HALF + k - 1
        total = wgl[around(-k if way == 0 else k), :, columns_of(which)]
        if k < first[which, way]:
            z_copy(which, way, k + 1).wait_recv()
            total = total + z_in[at + 1].astype(F32)
        z_out[at] = total.astype(BF16)
        z_copy(which, way, k).start()

    early = lax.div(around(HALF), RING // 2)
    shared(0)
    near_rows(early)
    near_rows(1 - early)
    shared(1)
    shared(2)
    far_rows(early)
    hop(0, 0, 4)
    hop(1, 1, 4)

    s1.wait_recv()
    s_half[...] = (s_own[:, lanes(core * width, width)].astype(F32) + s_core[...].astype(F32)).astype(BF16)
    s2 = send(s_half.at[:, lanes((1 - y) * quarter, quarter)], s_y, s_send.at[1], s_recv.at[1], other_y)
    s2.start()

    far_rows(1 - early)
    hop(0, 1, 3)
    hop(1, 0, 3)
    hop(0, 0, 3)
    hop(1, 1, 3)

    s2.wait_recv()
    s_z[z] = (s_half[:, lanes(y * quarter, quarter)].astype(F32) + s_y[...].astype(F32)).astype(BF16)

    def s_copy(k):
        return send(s_z.at[z], s_z.at[z], s_send.at[2], s_recv.at[2], peer(y, around(k), core))

    for k in range(1, RING):
        s_copy(k).start()

    for k in (2, 1):
        hop(0, 1, k)
        hop(1, 0, k)
        hop(0, 0, k)
        hop(1, 1, k)

    send(s_z.at[pl.ds(0, RING - 1)], s_z.at[pl.ds(0, RING - 1)], s_send.at[2], s_recv.at[2], other_y).wait_recv()
    fin = s_z[0].astype(F32)
    for k in range(1, RING):
        fin = fin + s_z[k].astype(F32)
    s_fin[:, lanes(y * quarter, quarter)] = fin.astype(BF16)
    mine = s_fin.at[:, lanes(y * quarter, quarter)]
    s4 = send(mine, s_fin.at[:, lanes(y * quarter, quarter)], s_send.at[3], s_recv.at[3], other_y)
    s4.start()

    for which in (0, 1):
        total = wgl[z, :, columns_of(which)]
        for way in (0, 1):
            z_copy(which, way, 1).wait_recv()
            total = total + z_in[(which * 2 + way) * HALF].astype(F32)
        final[:, :, columns_of(which)] = total.reshape(2, rows_own, quarter)
    last_out[...] = final[1 - core].astype(BF16)
    last_copy = send(last_out, last_in, last_sem.at[0], last_sem.at[1], other_core)
    last_copy.start()
    wg_ref[:, lanes(core * width, width)] = final[core]

    s4.wait_recv()
    s5 = send(s_fin, s_got, s_send.at[4], s_recv.at[4], other_core)
    s5.start()
    last_copy.wait_recv()
    wg_ref[:, lanes((1 - core) * width, width)] = last_in[...].astype(F32)

    s5.wait_recv()
    s_back[:, lanes(core * width, width)] = s_fin[...].astype(F32)
    s_back[:, lanes((1 - core) * width, width)] = s_got[...].astype(F32)
    for k in range(taps):
        kgrad_ref[k] = s_back[k : k + 1, :]
    ggrad_ref[...] = s_back[taps : taps + 1, :]

    s1.wait_send()
    s2.wait_send()
    send(s_z.at[pl.ds(0, RING - 1)], s_z.at[pl.ds(0, RING - 1)], s_send.at[2], s_recv.at[2], other_y).wait_send()
    s4.wait_send()
    s5.wait_send()
    last_copy.wait_send()
    send(act_in, act_in, act_send, act_recv.at[0], other_core).wait_send()
    send(gp_in, gp_in, gp_send, gp_recv.at[0], other_core).wait_send()
    for (which, way), start in first.items():
        for k in range(1, start + 1):
            z_copy(which, way, k).wait_send()

    @pl.when(me == last)
    def _():
        give(out_ref, hout[n_block - per : n_block])

    @pl.when(me == 0)
    def _():
        give(igrad_ref, gout[0:per])

    @pl.when(me != 0)
    def _():
        for i in range(per):
            send(irecv.at[i], irecv.at[i], b_send.at[i], i_recv.at[i], 0).wait_recv()
        give(igrad_ref, irecv[...])

    @pl.when(me != 0)
    def _():
        send(xin, xin, x_send, o_recv.at[0], 0).wait_send()

    @pl.when(me != last)
    def _():
        send(cin, cin, c_send, o_recv.at[0], 0).wait_send()

    def sent(b, carry):
        @pl.when((me != last) | (b < n_block - per))
        def _():
            send(hout.at[b], hist.at[b], f_send.at[b], f_recv.at[b], 0).wait_send()

        @pl.when((me != 0) | (b >= per))
        def _():
            send(gout.at[b], gin.at[b], b_send.at[b], b_recv.at[b], 0).wait_send()

        return carry

    lax.fori_loop(0, n_block, sent, 0)


def pipeline(x, lengths, cot, weight, kern, gain):
    sections = lax.axis_size("section")
    frames, feature = x.shape
    taps = kern.shape[0]
    n_block = sections * frames // BLOCK
    per = frames // BLOCK
    vmem = pl.BlockSpec(memory_space=pltpu.VMEM)
    anywhere = pl.BlockSpec(memory_space=pl.ANY)
    rows_own = feature // lax.axis_size("dp")
    blocks = (n_block, BLOCK, feature)
    own = (per, BLOCK, feature)
    return pl.pallas_call(
        functools.partial(kernel, sections, frames, taps, n_block),
        out_shape=(
            jax.ShapeDtypeStruct((frames, feature), BF16),
            jax.ShapeDtypeStruct((frames, feature), BF16),
            jax.ShapeDtypeStruct((rows_own, feature), F32),
            jax.ShapeDtypeStruct((taps, 1, feature), F32),
            jax.ShapeDtypeStruct((1, feature), F32),
        ),
        in_specs=[
            anywhere, pl.BlockSpec(memory_space=pltpu.SMEM), anywhere, anywhere, anywhere, anywhere,
        ],
        out_specs=(vmem, vmem, vmem, vmem, vmem),
        scratch_shapes=[
            pltpu.VMEM((frames, feature), BF16),
            pltpu.VMEM((frames, feature), BF16),
            pltpu.VMEM((taps, 1, feature), F32),
            pltpu.VMEM((1, feature), F32),
            pltpu.VMEM((feature, feature), BF16),
            pltpu.VMEM((feature, feature), BF16),
            pltpu.VMEM(blocks, BF16),
            pltpu.VMEM(blocks, BF16),
            pltpu.VMEM((n_block + 1, BLOCK, feature), F32),
            pltpu.VMEM(blocks, F32),
            pltpu.VMEM(blocks, BF16),
            pltpu.VMEM((n_block, BLOCK, 128), F32),
            pltpu.VMEM(blocks, BF16),
            pltpu.VMEM(blocks, BF16),
            pltpu.VMEM(blocks, BF16),
            pltpu.VMEM((n_block + 1, BLOCK, feature), F32),
            pltpu.VMEM((BLOCK, feature), F32),
            pltpu.VMEM((taps, 8, feature), F32),
            pltpu.VMEM((taps, 8, feature), F32),
            pltpu.VMEM((8, feature), F32),
            pltpu.VMEM(own, BF16),
            pltpu.VMEM(own, BF16),
            pltpu.VMEM(own, BF16),
            pltpu.VMEM(own, BF16),
            pltpu.VMEM((3, n_block, BLOCK, feature // 2), BF16),
            pltpu.VMEM((3, n_block, BLOCK, feature // 2), BF16),
            pltpu.VMEM((RING, 2 * rows_own, feature // 2), F32),
            pltpu.VMEM((4 * HALF, 2 * rows_own, feature // 4), BF16),
            pltpu.VMEM((4 * HALF, 2 * rows_own, feature // 4), BF16),
            pltpu.VMEM((2, rows_own, feature // 2), F32),
            pltpu.VMEM((rows_own, feature // 2), BF16),
            pltpu.VMEM((rows_own, feature // 2), BF16),
            pltpu.VMEM((taps + 1, feature), BF16),
            pltpu.VMEM((taps + 1, feature // 2), BF16),
            pltpu.VMEM((taps + 1, feature // 2), BF16),
            pltpu.VMEM((taps + 1, feature // 4), BF16),
            pltpu.VMEM((RING, taps + 1, feature // 4), BF16),
            pltpu.VMEM((taps + 1, feature // 2), BF16),
            pltpu.VMEM((taps + 1, feature // 2), BF16),
            pltpu.VMEM((taps + 1, feature), F32),
            pltpu.SemaphoreType.DMA,
            pltpu.SemaphoreType.DMA((4,)),
            pltpu.SemaphoreType.DMA((n_block,)),
            pltpu.SemaphoreType.DMA((n_block,)),
            pltpu.SemaphoreType.DMA((n_block,)),
            pltpu.SemaphoreType.DMA((n_block,)),
            pltpu.SemaphoreType.DMA,
            pltpu.SemaphoreType.DMA,
            pltpu.SemaphoreType.DMA((per,)),
            pltpu.SemaphoreType.DMA((per,)),
            pltpu.SemaphoreType.DMA,
            pltpu.SemaphoreType.DMA((3,)),
            pltpu.SemaphoreType.DMA,
            pltpu.SemaphoreType.DMA((3,)),
            pltpu.SemaphoreType.DMA((4 * HALF,)),
            pltpu.SemaphoreType.DMA((4 * HALF,)),
            pltpu.SemaphoreType.DMA((2,)),
            pltpu.SemaphoreType.DMA((5,)),
            pltpu.SemaphoreType.DMA((5,)),
        ],
        compiler_params=pltpu.CompilerParams(
            collective_id=0, has_side_effects=True, vmem_limit_bytes=60 * 1024 * 1024
        ),
        cost_estimate=pl.CostEstimate(
            flops=6 * n_block * BLOCK * feature * feature, bytes_accessed=4 * feature * feature, transcendentals=0
        ),
    )(x, lengths, cot, weight, kern, gain)


def hand_over(*refs):
    count = len(refs) // 2
    for taken, given in zip(refs[:count], refs[count:]):
        given[...] = taken[...]


def local(inputs, lengths, cotangent, weight, kern, gain):
    results = pipeline(inputs[0], lengths, cotangent[0], weight[0], jnp.transpose(kern, (1, 0, 2)), gain)
    vmem = pl.BlockSpec(memory_space=pltpu.VMEM)
    out, igrad, wg, kgrad, ggrad = pl.pallas_call(
        hand_over,
        out_shape=tuple(jax.ShapeDtypeStruct(r.shape, r.dtype) for r in results),
        in_specs=[vmem] * len(results),
        out_specs=(vmem,) * len(results),
    )(*results)
    return (out[None], igrad[None], wg[None], jnp.transpose(kgrad, (1, 0, 2)), ggrad)


def solution(mesh):
    return jax.shard_map(
        local,
        mesh=mesh,
        in_specs=(
            P("dp", "section", None),
            P("dp"),
            P("dp", "section", None),
            P("section", None, None),
            P("section", None, None),
            P("section", None),
        ),
        out_specs=(
            P("dp", "section", None),
            P("dp", "section", None),
            P("section", "dp", None),
            P("section", None, None),
            P("section", None),
        ),
        check_vma=False,
    )
```

```python
import functools

import jax
import jax.numpy as jnp
from jax import lax
from jax.experimental import pallas as pl
from jax.experimental.pallas import tpu as pltpu
from jax.sharding import PartitionSpec as P

EPSILON = 1e-05
BLOCK = 16
COLUMNS = 256
F32 = jnp.float32
BF16 = jnp.bfloat16


def order_matrix(frames, block, back):
    groups = block // 8
    row = lax.broadcasted_iota(jnp.int32, (frames, frames), 0)
    col = lax.broadcasted_iota(jnp.int32, (frames, frames), 1)
    kept, time = (col, row) if back else (row, col)
    inside = lax.rem(kept, block)
    frame = kept - inside + groups * lax.rem(inside, 8) + lax.div(inside, 8)
    return (frame == time).astype(BF16)


RING = 8
HALF = 4


def kernel(
    sections, frames, taps, n_block,
    x_hbm, len_ref, cot_hbm, w_hbm, kern_hbm, gain_hbm,
    out_ref, igrad_ref, wg_ref, kgrad_ref, ggrad_ref,
    x_ref, cot_ref, kern_ref, gain_ref, w, wt, hist, hout, normed, slope, act, inv, gin, gout, gp, gc, gh, kb, kacc, gacc, xin, cin, orecv, irecv,
    act_in, gp_in, wgl, z_out, z_in, final, last_out, last_in, s_own, s_core, s_half, s_y, s_z, s_fin, s_got, s_back,
    w_sem, arg_sems, f_recv, f_send, b_recv, b_send, x_send, c_send, o_recv, i_recv,
    act_send, act_recv, gp_send, gp_recv, z_send, z_recv, last_sem, s_send, s_recv,
):
    me = lax.axis_index("section")
    last = sections - 1
    feature = x_ref.shape[1]
    per = frames // BLOCK
    groups = BLOCK // 8
    halo = taps - 1

    dp = lax.axis_index("dp")
    core = lax.rem(dp, 2)
    z = lax.rem(lax.div(dp, 2), RING)
    y = lax.div(dp, 2 * RING)

    def around(offset):
        return lax.rem(z + offset + RING, RING)

    def peer(y_at, z_at, core_at):
        return {"dp": (y_at * RING + z_at) * 2 + core_at}

    other_core = peer(y, z, 1 - core)
    other_y = peer(1 - y, z, core)
    cross = peer(1 - y, z, 1 - core)

    barrier = pltpu.get_barrier_semaphore()
    partners = [{"section": lax.rem(me + d, sections)} for d in range(1, sections)]
    partners += [peer(y, around(d), core) for d in range(1, RING)] + [other_core, other_y, cross]
    for partner in partners:
        pl.semaphore_signal(barrier, inc=1, device_id=partner, device_id_type=pl.DeviceIdType.MESH)

    def strip(i):
        return pl.ds(pl.multiple_of(i * COLUMNS, COLUMNS), COLUMNS)

    def w_copy(i):
        return pltpu.make_async_copy(w_hbm.at[strip(i), :], w.at[strip(i), :], w_sem.at[i])

    arg_copies = [
        pltpu.make_async_copy(source, ref, arg_sems.at[i])
        for i, (source, ref) in enumerate(
            [(x_hbm, x_ref), (cot_hbm, cot_ref), (kern_hbm, kern_ref), (gain_hbm, gain_ref)]
        )
    ]
    for copy in arg_copies:
        copy.start()
    for i in range(feature // COLUMNS):
        w_copy(i).start()
    for copy in arg_copies:
        copy.wait()

    to_kept = order_matrix(frames, BLOCK, False)
    xin[...] = jnp.dot(to_kept, x_ref[...], preferred_element_type=F32).astype(BF16).reshape(xin.shape)
    cin[...] = jnp.dot(to_kept, cot_ref[...], preferred_element_type=F32).astype(BF16).reshape(cin.shape)

    for k in range(taps):
        kb[k] = jnp.broadcast_to(kern_ref[k], (8, feature))
    normed[0] = jnp.zeros_like(normed[0])
    gc[n_block] = jnp.zeros_like(gc[n_block])
    kacc[...] = jnp.zeros_like(kacc)
    gacc[...] = jnp.zeros_like(gacc)

    @pl.when(me == 0)
    def _():
        for i in range(per):
            hist[i] = xin[i]

    @pl.when(me == last)
    def _():
        for i in range(per):
            gin[n_block - per + i] = cin[i]

    def turn(i, carry):
        w_copy(i).wait()
        wt[:, strip(i)] = w[strip(i), :].T
        return carry

    lax.fori_loop(0, feature // COLUMNS, turn, 0)
    pl.semaphore_wait(barrier, len(partners))

    def send(src, dst, send_sem, recv_sem, to):
        return pltpu.make_async_remote_copy(
            src_ref=src, dst_ref=dst, send_sem=send_sem, recv_sem=recv_sem,
            device_id=to if isinstance(to, dict) else {"section": to}, device_id_type=pl.DeviceIdType.MESH,
        )

    def x_copy(i):
        return send(xin.at[i], hist.at[me * per + i], x_send, f_recv.at[me * per + i], 0)

    def c_copy(i):
        return send(cin.at[i], gin.at[me * per + i], c_send, b_recv.at[me * per + i], last)

    @pl.when(me != 0)
    def _():
        for i in range(per):
            x_copy(i).start()

    @pl.when(me != last)
    def _():
        for i in reversed(range(per)):
            c_copy(i).start()

    width = feature // 2
    quarter = feature // 4

    def lanes(start, size):
        return pl.ds(pl.multiple_of(start, 128), size)

    def share_act(b, slot, to, half):
        send(act.at[b, :, lanes(half * width, width)], act_in.at[slot, b], act_send, act_recv.at[slot], to).start()

    def share_gp(b):
        for slot, to, half in ((2, cross, 1 - y), (1, other_y, 1 - y), (0, other_core, y)):
            send(gp.at[b, :, lanes(half * width, width)], gp_in.at[slot, b], gp_send, gp_recv.at[slot], to).start()

    sub = lax.broadcasted_iota(jnp.int32, (8, COLUMNS), 0)
    length = len_ref[0]

    def valid_rows(b):
        row = lax.broadcasted_iota(jnp.int32, (BLOCK, 1), 0)
        frame = b * BLOCK + groups * lax.rem(row, 8) + lax.div(row, 8)
        return frame < length

    column_slices = [slice(c, c + COLUMNS) for c in range(0, feature, COLUMNS)]

    def forward(b, carry):
        @pl.when((me != 0) | (b >= per))
        def _():
            send(hist.at[b], hist.at[b], f_send.at[b], f_recv.at[b], 0).wait_recv()

        wide = hist[b].astype(F32)
        inverse = lax.rsqrt(jnp.sum(wide * wide, axis=1, keepdims=True) * (1.0 / feature) + EPSILON)
        inv[b] = jnp.broadcast_to(inverse, (BLOCK, 128))
        projected = None
        for cols in column_slices:
            fresh = (wide[:, cols] * inverse) * gain_ref[:, cols]
            normed[b + 1, :, cols] = fresh
            now = [fresh[8 * r : 8 * r + 8] for r in range(groups)]
            past = [normed[b, 8 * r : 8 * r + 8, cols] for r in range(groups)]
            shifted = {r: now[r] for r in range(groups)}
            for m in range(1, halo + 1):
                q = -(-m // groups)
                r = q * groups - m
                shifted[-m] = pltpu.roll(jnp.where(sub >= 8 - q, past[r], now[r]), q, 0)
            total = [None] * groups
            for k in range(taps):
                tap = kb[k, :, cols]
                for r in range(groups):
                    term = tap * shifted[r - halo + k]
                    total[r] = term if k == 0 else total[r] + term
            mixed = jnp.concatenate(total, axis=0)
            sigma = 0.5 * jnp.tanh(0.5 * mixed) + 0.5
            product = mixed * sigma
            slope[b, :, cols] = sigma + product * (1.0 - sigma)
            activated = product.astype(BF16)
            act[b, :, cols] = activated
            part = jnp.dot(activated, wt[cols, :], preferred_element_type=F32)
            projected = part if projected is None else projected + part
        hout[b] = (wide + jnp.where(valid_rows(b), projected, 0.0)).astype(BF16)

        to = jnp.minimum(me + 1, last)
        holder = lax.div(b, per)

        @pl.when(me != last)
        def _():
            send(hout.at[b], hist.at[b], f_send.at[b], f_recv.at[b], to).start()

        @pl.when((me == last) & (holder != last))
        def _():
            send(hout.at[b], orecv.at[lax.rem(b, per)], f_send.at[b], o_recv.at[lax.rem(b, per)], holder).start()

        share_act(b, 0, other_core, 1 - core)
        share_act(b, 1, other_y, core)
        share_act(b, 2, cross, 1 - core)
        return carry

    lax.fori_loop(0, n_block, forward, 0)

    from_kept = order_matrix(frames, BLOCK, True)

    def give(ref, rows):
        ref[...] = jnp.dot(from_kept, rows.reshape(frames, feature), preferred_element_type=F32).astype(BF16)

    @pl.when(me != last)
    def _():
        for i in range(per):
            send(orecv.at[i], orecv.at[i], f_send.at[i], o_recv.at[i], 0).wait_recv()
        give(out_ref, orecv[...])

    def backward(step, carry):
        b = n_block - 1 - step

        @pl.when((me != last) | (b < n_block - per))
        def _():
            send(gin.at[b], gin.at[b], b_send.at[b], b_recv.at[b], 0).wait_recv()

        grad = gin[b].astype(F32)
        masked = jnp.where(valid_rows(b), grad, 0.0).astype(BF16)
        gp[b] = masked

        @pl.when(b == 0)
        def _():
            share_gp(b)

        inverse = inv[b, :, 0:1]
        sums = jnp.zeros((BLOCK, 128), F32)
        for cols in column_slices:
            fresh = jnp.dot(masked, w[:, cols], preferred_element_type=F32) * slope[b, :, cols]
            gc[b, :, cols] = fresh
            now = [fresh[8 * r : 8 * r + 8] for r in range(groups)]
            later = [gc[b + 1, 8 * r : 8 * r + 8, cols] for r in range(groups)]
            shifted = {r: now[r] for r in range(groups)}
            for e in range(groups, groups + halo):
                q, r = divmod(e, groups)
                shifted[e] = pltpu.roll(jnp.where(sub < q, later[r], now[r]), 8 - q, 0)
            base = [normed[b + 1, 8 * r : 8 * r + 8, cols] for r in range(groups)]
            total = [None] * groups
            for k in range(taps):
                tap = kb[k, :, cols]
                grown = kacc[k, :, cols]
                for r in range(groups):
                    value = shifted[r + halo - k]
                    term = tap * value
                    total[r] = term if k == 0 else total[r] + term
                    grown = grown + value * base[r]
                kacc[k, :, cols] = grown
            grad_n = jnp.concatenate(total, axis=0)
            scaled = hist[b, :, cols].astype(F32) * inverse
            product = grad_n * scaled
            for r in range(groups):
                gacc[:, cols] += product[8 * r : 8 * r + 8]
            gh[:, cols] = grad_n * gain_ref[:, cols]
            product = product * gain_ref[:, cols]
            for p in range(0, COLUMNS, 128):
                sums = sums + product[:, p : p + 128]

        mean = jnp.sum(sums, axis=1, keepdims=True) * (1.0 / feature)
        scaled = hist[b].astype(F32) * inverse
        gout[b] = (gin[b].astype(F32) + inverse * (gh[...] - scaled * mean)).astype(BF16)

        to = jnp.maximum(me - 1, 0)
        holder = lax.div(b, per)

        @pl.when(me != 0)
        def _():
            send(gout.at[b], gin.at[b], b_send.at[b], b_recv.at[b], to).start()

        @pl.when((me == 0) & (holder != 0))
        def _():
            send(gout.at[b], irecv.at[lax.rem(b, per)], b_send.at[b], i_recv.at[lax.rem(b, per)], holder).start()

        @pl.when(b != 0)
        def _():
            share_gp(b)

        return carry

    lax.fori_loop(0, n_block, backward, 0)

    rows_own = feature // (4 * RING)
    total_frames = n_block * BLOCK
    batch = width // 2

    s_own[0:taps, :] = jnp.sum(kacc[...], axis=1).astype(BF16)
    s_own[taps : taps + 1, :] = jnp.sum(gacc[...], axis=0, keepdims=True).astype(BF16)
    s1 = send(s_own.at[:, lanes((1 - core) * width, width)], s_core, s_send.at[0], s_recv.at[0], other_core)
    s1.start()

    def shared(slot):
        send(act_in.at[slot], act_in.at[slot], act_send, act_recv.at[slot], other_core).wait_recv()
        send(gp_in.at[slot], gp_in.at[slot], gp_send, gp_recv.at[slot], other_core).wait_recv()

    def product(left, right):
        return lax.dot_general(
            left.reshape(total_frames, batch), right.reshape(total_frames, width),
            (((0,), (0,)), ((), ())), preferred_element_type=F32,
        )

    def rows_of(j):
        return pl.ds(j * (RING // 2), RING // 2)

    def near_rows(j):
        part = product(gp[:, :, lanes(y * width + j * batch, batch)], act[:, :, lanes(core * width, width)])
        part = part + product(gp_in[0, :, :, lanes(j * batch, batch)], act_in[0])
        wgl[rows_of(j)] = part.reshape(RING // 2, 2 * rows_own, width)

    def far_rows(j):
        part = product(gp_in[1, :, :, lanes(j * batch, batch)], act_in[1])
        part = part + product(gp_in[2, :, :, lanes(j * batch, batch)], act_in[2])
        wgl[rows_of(j)] += part.reshape(RING // 2, 2 * rows_own, width)

    first = {(0, 0): HALF, (0, 1): HALF - 1, (1, 0): HALF - 1, (1, 1): HALF}

    def columns_of(which):
        return slice(which * quarter, (which + 1) * quarter)

    def z_copy(which, way, k):
        at = (which * 2 + way) * HALF + k - 1
        step = -1 if way == 0 else 1
        return send(z_out.at[at], z_in.at[at], z_send.at[at], z_recv.at[at], peer(y, around(step), core))

    def hop(which, way, k):
        at = (which * 2 + way) * HALF + k - 1
        total = wgl[around(-k if way == 0 else k), :, columns_of(which)]
        if k < first[which, way]:
            z_copy(which, way, k + 1).wait_recv()
            total = total + z_in[at + 1].astype(F32)
        z_out[at] = total.astype(BF16)
        z_copy(which, way, k).start()

    early = lax.div(around(HALF), RING // 2)
    shared(0)
    near_rows(early)
    near_rows(1 - early)
    shared(1)
    shared(2)
    far_rows(early)
    hop(0, 0, 4)
    hop(1, 1, 4)

    s1.wait_recv()
    s_half[...] = (s_own[:, lanes(core * width, width)].astype(F32) + s_core[...].astype(F32)).astype(BF16)
    s2 = send(s_half.at[:, lanes((1 - y) * quarter, quarter)], s_y, s_send.at[1], s_recv.at[1], other_y)
    s2.start()

    far_rows(1 - early)
    hop(0, 1, 3)
    hop(1, 0, 3)
    hop(0, 0, 3)
    hop(1, 1, 3)

    s2.wait_recv()
    s_z[z] = (s_half[:, lanes(y * quarter, quarter)].astype(F32) + s_y[...].astype(F32)).astype(BF16)

    def s_copy(k):
        return send(s_z.at[z], s_z.at[z], s_send.at[2], s_recv.at[2], peer(y, around(k), core))

    for k in range(1, RING):
        s_copy(k).start()

    @pl.when(me == last)
    def _():
        give(out_ref, hout[n_block - per : n_block])

    @pl.when(me == 0)
    def _():
        give(igrad_ref, gout[0:per])

    for k in (2, 1):
        hop(0, 1, k)
        hop(1, 0, k)
        hop(0, 0, k)
        hop(1, 1, k)

    send(s_z.at[pl.ds(0, RING - 1)], s_z.at[pl.ds(0, RING - 1)], s_send.at[2], s_recv.at[2], other_y).wait_recv()
    fin = s_z[0].astype(F32)
    for k in range(1, RING):
        fin = fin + s_z[k].astype(F32)
    s_fin[:, lanes(y * quarter, quarter)] = fin.astype(BF16)
    mine = s_fin.at[:, lanes(y * quarter, quarter)]
    s4 = send(mine, s_fin.at[:, lanes(y * quarter, quarter)], s_send.at[3], s_recv.at[3], other_y)
    s4.start()

    for which in (0, 1):
        total = wgl[z, :, columns_of(which)]
        for way in (0, 1):
            z_copy(which, way, 1).wait_recv()
            total = total + z_in[(which * 2 + way) * HALF].astype(F32)
        final[:, :, columns_of(which)] = total.reshape(2, rows_own, quarter)
    last_out[...] = final[1 - core].astype(BF16)
    last_copy = send(last_out, last_in, last_sem.at[0], last_sem.at[1], other_core)
    last_copy.start()
    wg_ref[:, lanes(core * width, width)] = final[core]

    s4.wait_recv()
    s5 = send(s_fin, s_got, s_send.at[4], s_recv.at[4], other_core)
    s5.start()
    last_copy.wait_recv()
    wg_ref[:, lanes((1 - core) * width, width)] = last_in[...].astype(F32)

    s5.wait_recv()
    s_back[:, lanes(core * width, width)] = s_fin[...].astype(F32)
    s_back[:, lanes((1 - core) * width, width)] = s_got[...].astype(F32)
    for k in range(taps):
        kgrad_ref[k] = s_back[k : k + 1, :]
    ggrad_ref[...] = s_back[taps : taps + 1, :]

    s1.wait_send()
    s2.wait_send()
    send(s_z.at[pl.ds(0, RING - 1)], s_z.at[pl.ds(0, RING - 1)], s_send.at[2], s_recv.at[2], other_y).wait_send()
    s4.wait_send()
    s5.wait_send()
    last_copy.wait_send()
    send(act_in, act_in, act_send, act_recv.at[0], other_core).wait_send()
    send(gp_in, gp_in, gp_send, gp_recv.at[0], other_core).wait_send()
    for (which, way), start in first.items():
        for k in range(1, start + 1):
            z_copy(which, way, k).wait_send()

    @pl.when(me != 0)
    def _():
        for i in range(per):
            send(irecv.at[i], irecv.at[i], b_send.at[i], i_recv.at[i], 0).wait_recv()
        give(igrad_ref, irecv[...])

    @pl.when(me != 0)
    def _():
        send(xin, xin, x_send, o_recv.at[0], 0).wait_send()

    @pl.when(me != last)
    def _():
        send(cin, cin, c_send, o_recv.at[0], 0).wait_send()

    def sent(b, carry):
        @pl.when((me != last) | (b < n_block - per))
        def _():
            send(hout.at[b], hist.at[b], f_send.at[b], f_recv.at[b], 0).wait_send()

        @pl.when((me != 0) | (b >= per))
        def _():
            send(gout.at[b], gin.at[b], b_send.at[b], b_recv.at[b], 0).wait_send()

        return carry

    lax.fori_loop(0, n_block, sent, 0)


def pipeline(x, lengths, cot, weight, kern, gain):
    sections = lax.axis_size("section")
    frames, feature = x.shape
    taps = kern.shape[0]
    n_block = sections * frames // BLOCK
    per = frames // BLOCK
    vmem = pl.BlockSpec(memory_space=pltpu.VMEM)
    anywhere = pl.BlockSpec(memory_space=pl.ANY)
    rows_own = feature // lax.axis_size("dp")
    blocks = (n_block, BLOCK, feature)
    own = (per, BLOCK, feature)
    return pl.pallas_call(
        functools.partial(kernel, sections, frames, taps, n_block),
        out_shape=(
            jax.ShapeDtypeStruct((frames, feature), BF16),
            jax.ShapeDtypeStruct((frames, feature), BF16),
            jax.ShapeDtypeStruct((rows_own, feature), F32),
            jax.ShapeDtypeStruct((taps, 1, feature), F32),
            jax.ShapeDtypeStruct((1, feature), F32),
        ),
        in_specs=[
            anywhere, pl.BlockSpec(memory_space=pltpu.SMEM), anywhere, anywhere, anywhere, anywhere,
        ],
        out_specs=(vmem, vmem, vmem, vmem, vmem),
        scratch_shapes=[
            pltpu.VMEM((frames, feature), BF16),
            pltpu.VMEM((frames, feature), BF16),
            pltpu.VMEM((taps, 1, feature), F32),
            pltpu.VMEM((1, feature), F32),
            pltpu.VMEM((feature, feature), BF16),
            pltpu.VMEM((feature, feature), BF16),
            pltpu.VMEM(blocks, BF16),
            pltpu.VMEM(blocks, BF16),
            pltpu.VMEM((n_block + 1, BLOCK, feature), F32),
            pltpu.VMEM(blocks, F32),
            pltpu.VMEM(blocks, BF16),
            pltpu.VMEM((n_block, BLOCK, 128), F32),
            pltpu.VMEM(blocks, BF16),
            pltpu.VMEM(blocks, BF16),
            pltpu.VMEM(blocks, BF16),
            pltpu.VMEM((n_block + 1, BLOCK, feature), F32),
            pltpu.VMEM((BLOCK, feature), F32),
            pltpu.VMEM((taps, 8, feature), F32),
            pltpu.VMEM((taps, 8, feature), F32),
            pltpu.VMEM((8, feature), F32),
            pltpu.VMEM(own, BF16),
            pltpu.VMEM(own, BF16),
            pltpu.VMEM(own, BF16),
            pltpu.VMEM(own, BF16),
            pltpu.VMEM((3, n_block, BLOCK, feature // 2), BF16),
            pltpu.VMEM((3, n_block, BLOCK, feature // 2), BF16),
            pltpu.VMEM((RING, 2 * rows_own, feature // 2), F32),
            pltpu.VMEM((4 * HALF, 2 * rows_own, feature // 4), BF16),
            pltpu.VMEM((4 * HALF, 2 * rows_own, feature // 4), BF16),
            pltpu.VMEM((2, rows_own, feature // 2), F32),
            pltpu.VMEM((rows_own, feature // 2), BF16),
            pltpu.VMEM((rows_own, feature // 2), BF16),
            pltpu.VMEM((taps + 1, feature), BF16),
            pltpu.VMEM((taps + 1, feature // 2), BF16),
            pltpu.VMEM((taps + 1, feature // 2), BF16),
            pltpu.VMEM((taps + 1, feature // 4), BF16),
            pltpu.VMEM((RING, taps + 1, feature // 4), BF16),
            pltpu.VMEM((taps + 1, feature // 2), BF16),
            pltpu.VMEM((taps + 1, feature // 2), BF16),
            pltpu.VMEM((taps + 1, feature), F32),
            pltpu.SemaphoreType.DMA((feature // COLUMNS,)),
            pltpu.SemaphoreType.DMA((4,)),
            pltpu.SemaphoreType.DMA((n_block,)),
            pltpu.SemaphoreType.DMA((n_block,)),
            pltpu.SemaphoreType.DMA((n_block,)),
            pltpu.SemaphoreType.DMA((n_block,)),
            pltpu.SemaphoreType.DMA,
            pltpu.SemaphoreType.DMA,
            pltpu.SemaphoreType.DMA((per,)),
            pltpu.SemaphoreType.DMA((per,)),
            pltpu.SemaphoreType.DMA,
            pltpu.SemaphoreType.DMA((3,)),
            pltpu.SemaphoreType.DMA,
            pltpu.SemaphoreType.DMA((3,)),
            pltpu.SemaphoreType.DMA((4 * HALF,)),
            pltpu.SemaphoreType.DMA((4 * HALF,)),
            pltpu.SemaphoreType.DMA((2,)),
            pltpu.SemaphoreType.DMA((5,)),
            pltpu.SemaphoreType.DMA((5,)),
        ],
        compiler_params=pltpu.CompilerParams(
            collective_id=0, has_side_effects=True, vmem_limit_bytes=60 * 1024 * 1024
        ),
        cost_estimate=pl.CostEstimate(
            flops=6 * n_block * BLOCK * feature * feature, bytes_accessed=4 * feature * feature, transcendentals=0
        ),
    )(x, lengths, cot, weight, kern, gain)


def hand_over(*refs):
    count = len(refs) // 2
    for taken, given in zip(refs[:count], refs[count:]):
        given[...] = taken[...]


def local(inputs, lengths, cotangent, weight, kern, gain):
    results = pipeline(inputs[0], lengths, cotangent[0], weight[0], jnp.transpose(kern, (1, 0, 2)), gain)
    vmem = pl.BlockSpec(memory_space=pltpu.VMEM)
    out, igrad, wg, kgrad, ggrad = pl.pallas_call(
        hand_over,
        out_shape=tuple(jax.ShapeDtypeStruct(r.shape, r.dtype) for r in results),
        in_specs=[vmem] * len(results),
        out_specs=(vmem,) * len(results),
    )(*results)
    return (out[None], igrad[None], wg[None], jnp.transpose(kgrad, (1, 0, 2)), ggrad)


def solution(mesh):
    return jax.shard_map(
        local,
        mesh=mesh,
        in_specs=(
            P("dp", "section", None),
            P("dp"),
            P("dp", "section", None),
            P("section", None, None),
            P("section", None, None),
            P("section", None),
        ),
        out_specs=(
            P("dp", "section", None),
            P("dp", "section", None),
            P("section", "dp", None),
            P("section", None, None),
            P("section", None),
        ),
        check_vma=False,
    )
```

```python
import functools

import jax
import jax.numpy as jnp
from jax import lax
from jax.experimental import pallas as pl
from jax.experimental.pallas import tpu as pltpu
from jax.sharding import PartitionSpec as P

EPSILON = 1e-05
BLOCK = 16
COLUMNS = 256
F32 = jnp.float32
BF16 = jnp.bfloat16


def order_matrix(frames, block, back):
    groups = block // 8
    row = lax.broadcasted_iota(jnp.int32, (frames, frames), 0)
    col = lax.broadcasted_iota(jnp.int32, (frames, frames), 1)
    kept, time = (col, row) if back else (row, col)
    inside = lax.rem(kept, block)
    frame = kept - inside + groups * lax.rem(inside, 8) + lax.div(inside, 8)
    return (frame == time).astype(BF16)


RING = 8
HALF = 4


def kernel(
    sections, frames, taps, n_block,
    x_hbm, len_ref, cot_hbm, w_hbm, kern_hbm, gain_hbm,
    out_ref, igrad_ref, wg_ref, kgrad_ref, ggrad_ref,
    x_ref, cot_ref, kern_ref, gain_ref, w, wt, hist, hout, normed, slope, act, inv, gin, gout, gp, gc, gh, kb, kacc, gacc, xin, cin, orecv, irecv,
    act_in, gp_in, wgl, z_out, z_in, final, last_out, last_in, s_own, s_core, s_half, s_y, s_z, s_fin, s_got, s_back,
    w_sem, arg_sems, f_recv, f_send, b_recv, b_send, x_send, c_send, o_recv, i_recv,
    act_send, act_recv, gp_send, gp_recv, z_send, z_recv, last_sem, s_send, s_recv,
):
    me = lax.axis_index("section")
    last = sections - 1
    feature = x_ref.shape[1]
    per = frames // BLOCK
    groups = BLOCK // 8
    halo = taps - 1

    dp = lax.axis_index("dp")
    core = lax.rem(dp, 2)
    z = lax.rem(lax.div(dp, 2), RING)
    y = lax.div(dp, 2 * RING)

    def around(offset):
        return lax.rem(z + offset + RING, RING)

    def peer(y_at, z_at, core_at):
        return {"dp": (y_at * RING + z_at) * 2 + core_at}

    other_core = peer(y, z, 1 - core)
    other_y = peer(1 - y, z, core)
    cross = peer(1 - y, z, 1 - core)

    barrier = pltpu.get_barrier_semaphore()
    partners = [{"section": lax.rem(me + d, sections)} for d in range(1, sections)]
    partners += [peer(y, around(d), core) for d in range(1, RING)] + [other_core, other_y, cross]
    for partner in partners:
        pl.semaphore_signal(barrier, inc=1, device_id=partner, device_id_type=pl.DeviceIdType.MESH)

    w_copy = pltpu.make_async_copy(w_hbm, w, w_sem)
    arg_copies = [
        pltpu.make_async_copy(source, ref, arg_sems.at[i])
        for i, (source, ref) in enumerate(
            [(x_hbm, x_ref), (cot_hbm, cot_ref), (kern_hbm, kern_ref), (gain_hbm, gain_ref)]
        )
    ]
    for copy in arg_copies:
        copy.start()
    w_copy.start()
    for copy in arg_copies:
        copy.wait()

    to_kept = order_matrix(frames, BLOCK, False)
    xin[...] = jnp.dot(to_kept, x_ref[...], preferred_element_type=F32).astype(BF16).reshape(xin.shape)
    cin[...] = jnp.dot(to_kept, cot_ref[...], preferred_element_type=F32).astype(BF16).reshape(cin.shape)

    for k in range(taps):
        kb[k] = jnp.broadcast_to(kern_ref[k], (8, feature))
    normed[0] = jnp.zeros_like(normed[0])
    gc[n_block] = jnp.zeros_like(gc[n_block])
    kacc[...] = jnp.zeros_like(kacc)
    gacc[...] = jnp.zeros_like(gacc)

    @pl.when(me == 0)
    def _():
        for i in range(per):
            hist[i] = xin[i]

    @pl.when(me == last)
    def _():
        for i in range(per):
            gin[n_block - per + i] = cin[i]

    w_copy.wait()

    def turn(i, carry):
        strip = pl.ds(pl.multiple_of(i * COLUMNS, COLUMNS), COLUMNS)
        wt[:, strip] = w[strip, :].T
        return carry

    lax.fori_loop(0, feature // COLUMNS, turn, 0)
    pl.semaphore_wait(barrier, len(partners))

    def send(src, dst, send_sem, recv_sem, to):
        return pltpu.make_async_remote_copy(
            src_ref=src, dst_ref=dst, send_sem=send_sem, recv_sem=recv_sem,
            device_id=to if isinstance(to, dict) else {"section": to}, device_id_type=pl.DeviceIdType.MESH,
        )

    def x_copy(i):
        return send(xin.at[i], hist.at[me * per + i], x_send, f_recv.at[me * per + i], 0)

    def c_copy(i):
        return send(cin.at[i], gin.at[me * per + i], c_send, b_recv.at[me * per + i], last)

    @pl.when(me != 0)
    def _():
        for i in range(per):
            x_copy(i).start()

    @pl.when(me != last)
    def _():
        for i in reversed(range(per)):
            c_copy(i).start()

    width = feature // 2
    quarter = feature // 4

    def lanes(start, size):
        return pl.ds(pl.multiple_of(start, 128), size)

    def share_act(b, slot, to, half):
        send(act.at[b, :, lanes(half * width, width)], act_in.at[slot, b], act_send, act_recv.at[slot], to).start()

    def share_gp(b):
        for slot, to, half in ((2, cross, 1 - y), (1, other_y, 1 - y), (0, other_core, y)):
            send(gp.at[b, :, lanes(half * width, width)], gp_in.at[slot, b], gp_send, gp_recv.at[slot], to).start()

    sub = lax.broadcasted_iota(jnp.int32, (8, COLUMNS), 0)
    length = len_ref[0]

    def valid_rows(b):
        row = lax.broadcasted_iota(jnp.int32, (BLOCK, 1), 0)
        frame = b * BLOCK + groups * lax.rem(row, 8) + lax.div(row, 8)
        return frame < length

    column_slices = [slice(c, c + COLUMNS) for c in range(0, feature, COLUMNS)]

    def forward(b, carry):
        @pl.when((me != 0) | (b >= per))
        def _():
            send(hist.at[b], hist.at[b], f_send.at[b], f_recv.at[b], 0).wait_recv()

        wide = hist[b].astype(F32)
        inverse = lax.rsqrt(jnp.sum(wide * wide, axis=1, keepdims=True) * (1.0 / feature) + EPSILON)
        inv[b] = jnp.broadcast_to(inverse, (BLOCK, 128))
        projected = None
        for cols in column_slices:
            fresh = (wide[:, cols] * inverse) * gain_ref[:, cols]
            normed[b + 1, :, cols] = fresh
            now = [fresh[8 * r : 8 * r + 8] for r in range(groups)]
            past = [normed[b, 8 * r : 8 * r + 8, cols] for r in range(groups)]
            shifted = {r: now[r] for r in range(groups)}
            for m in range(1, halo + 1):
                q = -(-m // groups)
                r = q * groups - m
                shifted[-m] = pltpu.roll(jnp.where(sub >= 8 - q, past[r], now[r]), q, 0)
            total = [None] * groups
            for k in range(taps):
                tap = kb[k, :, cols]
                for r in range(groups):
                    term = tap * shifted[r - halo + k]
                    total[r] = term if k == 0 else total[r] + term
            mixed = jnp.concatenate(total, axis=0)
            sigma = 0.5 * jnp.tanh(0.5 * mixed) + 0.5
            product = mixed * sigma
            slope[b, :, cols] = sigma + product * (1.0 - sigma)
            activated = product.astype(BF16)
            act[b, :, cols] = activated
            part = jnp.dot(activated, wt[cols, :], preferred_element_type=F32)
            projected = part if projected is None else projected + part
        hout[b] = (wide + jnp.where(valid_rows(b), projected, 0.0)).astype(BF16)

        to = jnp.minimum(me + 1, last)
        holder = lax.div(b, per)

        @pl.when(me != last)
        def _():
            send(hout.at[b], hist.at[b], f_send.at[b], f_recv.at[b], to).start()

        @pl.when((me == last) & (holder != last))
        def _():
            send(hout.at[b], orecv.at[lax.rem(b, per)], f_send.at[b], o_recv.at[lax.rem(b, per)], holder).start()

        share_act(b, 2, cross, 1 - core)
        share_act(b, 1, other_y, core)
        share_act(b, 0, other_core, 1 - core)
        return carry

    lax.fori_loop(0, n_block, forward, 0)

    from_kept = order_matrix(frames, BLOCK, True)

    def give(ref, rows):
        ref[...] = jnp.dot(from_kept, rows.reshape(frames, feature), preferred_element_type=F32).astype(BF16)

    @pl.when(me != last)
    def _():
        for i in range(per):
            send(orecv.at[i], orecv.at[i], f_send.at[i], o_recv.at[i], 0).wait_recv()
        give(out_ref, orecv[...])

    def backward(step, carry):
        b = n_block - 1 - step

        @pl.when((me != last) | (b < n_block - per))
        def _():
            send(gin.at[b], gin.at[b], b_send.at[b], b_recv.at[b], 0).wait_recv()

        grad = gin[b].astype(F32)
        masked = jnp.where(valid_rows(b), grad, 0.0).astype(BF16)
        gp[b] = masked

        @pl.when(b == 0)
        def _():
            share_gp(b)

        inverse = inv[b, :, 0:1]
        sums = jnp.zeros((BLOCK, 128), F32)
        for cols in column_slices:
            fresh = jnp.dot(masked, w[:, cols], preferred_element_type=F32) * slope[b, :, cols]
            gc[b, :, cols] = fresh
            now = [fresh[8 * r : 8 * r + 8] for r in range(groups)]
            later = [gc[b + 1, 8 * r : 8 * r + 8, cols] for r in range(groups)]
            shifted = {r: now[r] for r in range(groups)}
            for e in range(groups, groups + halo):
                q, r = divmod(e, groups)
                shifted[e] = pltpu.roll(jnp.where(sub < q, later[r], now[r]), 8 - q, 0)
            base = [normed[b + 1, 8 * r : 8 * r + 8, cols] for r in range(groups)]
            total = [None] * groups
            for k in range(taps):
                tap = kb[k, :, cols]
                grown = kacc[k, :, cols]
                for r in range(groups):
                    value = shifted[r + halo - k]
                    term = tap * value
                    total[r] = term if k == 0 else total[r] + term
                    grown = grown + value * base[r]
                kacc[k, :, cols] = grown
            grad_n = jnp.concatenate(total, axis=0)
            scaled = hist[b, :, cols].astype(F32) * inverse
            product = grad_n * scaled
            for r in range(groups):
                gacc[:, cols] += product[8 * r : 8 * r + 8]
            gh[:, cols] = grad_n * gain_ref[:, cols]
            product = product * gain_ref[:, cols]
            for p in range(0, COLUMNS, 128):
                sums = sums + product[:, p : p + 128]

        mean = jnp.sum(sums, axis=1, keepdims=True) * (1.0 / feature)
        scaled = hist[b].astype(F32) * inverse
        gout[b] = (gin[b].astype(F32) + inverse * (gh[...] - scaled * mean)).astype(BF16)

        to = jnp.maximum(me - 1, 0)
        holder = lax.div(b, per)

        @pl.when(me != 0)
        def _():
            send(gout.at[b], gin.at[b], b_send.at[b], b_recv.at[b], to).start()

        @pl.when((me == 0) & (holder != 0))
        def _():
            send(gout.at[b], irecv.at[lax.rem(b, per)], b_send.at[b], i_recv.at[lax.rem(b, per)], holder).start()

        @pl.when(b != 0)
        def _():
            share_gp(b)

        return carry

    lax.fori_loop(0, n_block, backward, 0)

    rows_own = feature // (4 * RING)
    total_frames = n_block * BLOCK
    batch = width // 2

    s_own[0:taps, :] = jnp.sum(kacc[...], axis=1).astype(BF16)
    s_own[taps : taps + 1, :] = jnp.sum(gacc[...], axis=0, keepdims=True).astype(BF16)
    s1 = send(s_own.at[:, lanes((1 - core) * width, width)], s_core, s_send.at[0], s_recv.at[0], other_core)
    s1.start()

    def shared(slot):
        send(act_in.at[slot], act_in.at[slot], act_send, act_recv.at[slot], other_core).wait_recv()
        send(gp_in.at[slot], gp_in.at[slot], gp_send, gp_recv.at[slot], other_core).wait_recv()

    def product(left, right):
        return lax.dot_general(
            left.reshape(total_frames, batch), right.reshape(total_frames, width),
            (((0,), (0,)), ((), ())), preferred_element_type=F32,
        )

    def rows_of(j):
        return pl.ds(j * (RING // 2), RING // 2)

    def near_rows(j):
        part = product(gp[:, :, lanes(y * width + j * batch, batch)], act[:, :, lanes(core * width, width)])
        part = part + product(gp_in[0, :, :, lanes(j * batch, batch)], act_in[0])
        wgl[rows_of(j)] = part.reshape(RING // 2, 2 * rows_own, width)

    def far_rows(j):
        part = product(gp_in[1, :, :, lanes(j * batch, batch)], act_in[1])
        part = part + product(gp_in[2, :, :, lanes(j * batch, batch)], act_in[2])
        wgl[rows_of(j)] += part.reshape(RING // 2, 2 * rows_own, width)

    first = {(0, 0): HALF, (0, 1): HALF - 1, (1, 0): HALF - 1, (1, 1): HALF}

    def columns_of(which):
        return slice(which * quarter, (which + 1) * quarter)

    def z_copy(which, way, k):
        at = (which * 2 + way) * HALF + k - 1
        step = -1 if way == 0 else 1
        return send(z_out.at[at], z_in.at[at], z_send.at[at], z_recv.at[at], peer(y, around(step), core))

    def hop(which, way, k):
        at = (which * 2 + way) * HALF + k - 1
        total = wgl[around(-k if way == 0 else k), :, columns_of(which)]
        if k < first[which, way]:
            z_copy(which, way, k + 1).wait_recv()
            total = total + z_in[at + 1].astype(F32)
        z_out[at] = total.astype(BF16)
        z_copy(which, way, k).start()

    early = lax.div(around(HALF), RING // 2)
    shared(0)
    near_rows(early)
    near_rows(1 - early)
    shared(1)
    shared(2)
    far_rows(early)
    hop(0, 0, 4)
    hop(1, 1, 4)

    s1.wait_recv()
    s_half[...] = (s_own[:, lanes(core * width, width)].astype(F32) + s_core[...].astype(F32)).astype(BF16)
    s2 = send(s_half.at[:, lanes((1 - y) * quarter, quarter)], s_y, s_send.at[1], s_recv.at[1], other_y)
    s2.start()

    far_rows(1 - early)
    hop(0, 1, 3)
    hop(1, 0, 3)
    hop(0, 0, 3)
    hop(1, 1, 3)

    s2.wait_recv()
    s_z[z] = (s_half[:, lanes(y * quarter, quarter)].astype(F32) + s_y[...].astype(F32)).astype(BF16)

    def s_copy(k):
        return send(s_z.at[z], s_z.at[z], s_send.at[2], s_recv.at[2], peer(y, around(k), core))

    for k in range(1, RING):
        s_copy(k).start()

    for k in (2, 1):
        hop(0, 1, k)
        hop(1, 0, k)
        hop(0, 0, k)
        hop(1, 1, k)

    send(s_z.at[pl.ds(0, RING - 1)], s_z.at[pl.ds(0, RING - 1)], s_send.at[2], s_recv.at[2], other_y).wait_recv()
    fin = s_z[0].astype(F32)
    for k in range(1, RING):
        fin = fin + s_z[k].astype(F32)
    s_fin[:, lanes(y * quarter, quarter)] = fin.astype(BF16)
    mine = s_fin.at[:, lanes(y * quarter, quarter)]
    s4 = send(mine, s_fin.at[:, lanes(y * quarter, quarter)], s_send.at[3], s_recv.at[3], other_y)
    s4.start()

    for which in (0, 1):
        total = wgl[z, :, columns_of(which)]
        for way in (0, 1):
            z_copy(which, way, 1).wait_recv()
            total = total + z_in[(which * 2 + way) * HALF].astype(F32)
        final[:, :, columns_of(which)] = total.reshape(2, rows_own, quarter)
    last_out[...] = final[1 - core].astype(BF16)
    last_copy = send(last_out, last_in, last_sem.at[0], last_sem.at[1], other_core)
    last_copy.start()
    wg_ref[:, lanes(core * width, width)] = final[core]

    s4.wait_recv()
    s5 = send(s_fin, s_got, s_send.at[4], s_recv.at[4], other_core)
    s5.start()
    last_copy.wait_recv()
    wg_ref[:, lanes((1 - core) * width, width)] = last_in[...].astype(F32)

    s5.wait_recv()
    s_back[:, lanes(core * width, width)] = s_fin[...].astype(F32)
    s_back[:, lanes((1 - core) * width, width)] = s_got[...].astype(F32)
    for k in range(taps):
        kgrad_ref[k] = s_back[k : k + 1, :]
    ggrad_ref[...] = s_back[taps : taps + 1, :]

    s1.wait_send()
    s2.wait_send()
    send(s_z.at[pl.ds(0, RING - 1)], s_z.at[pl.ds(0, RING - 1)], s_send.at[2], s_recv.at[2], other_y).wait_send()
    s4.wait_send()
    s5.wait_send()
    last_copy.wait_send()
    send(act_in, act_in, act_send, act_recv.at[0], other_core).wait_send()
    send(gp_in, gp_in, gp_send, gp_recv.at[0], other_core).wait_send()
    for (which, way), start in first.items():
        for k in range(1, start + 1):
            z_copy(which, way, k).wait_send()

    @pl.when(me == last)
    def _():
        give(out_ref, hout[n_block - per : n_block])

    @pl.when(me == 0)
    def _():
        give(igrad_ref, gout[0:per])

    @pl.when(me != 0)
    def _():
        for i in range(per):
            send(irecv.at[i], irecv.at[i], b_send.at[i], i_recv.at[i], 0).wait_recv()
        give(igrad_ref, irecv[...])

    @pl.when(me != 0)
    def _():
        send(xin, xin, x_send, o_recv.at[0], 0).wait_send()

    @pl.when(me != last)
    def _():
        send(cin, cin, c_send, o_recv.at[0], 0).wait_send()

    def sent(b, carry):
        @pl.when((me != last) | (b < n_block - per))
        def _():
            send(hout.at[b], hist.at[b], f_send.at[b], f_recv.at[b], 0).wait_send()

        @pl.when((me != 0) | (b >= per))
        def _():
            send(gout.at[b], gin.at[b], b_send.at[b], b_recv.at[b], 0).wait_send()

        return carry

    lax.fori_loop(0, n_block, sent, 0)


def pipeline(x, lengths, cot, weight, kern, gain):
    sections = lax.axis_size("section")
    frames, feature = x.shape
    taps = kern.shape[0]
    n_block = sections * frames // BLOCK
    per = frames // BLOCK
    vmem = pl.BlockSpec(memory_space=pltpu.VMEM)
    anywhere = pl.BlockSpec(memory_space=pl.ANY)
    rows_own = feature // lax.axis_size("dp")
    blocks = (n_block, BLOCK, feature)
    own = (per, BLOCK, feature)
    return pl.pallas_call(
        functools.partial(kernel, sections, frames, taps, n_block),
        out_shape=(
            jax.ShapeDtypeStruct((frames, feature), BF16),
            jax.ShapeDtypeStruct((frames, feature), BF16),
            jax.ShapeDtypeStruct((rows_own, feature), F32),
            jax.ShapeDtypeStruct((taps, 1, feature), F32),
            jax.ShapeDtypeStruct((1, feature), F32),
        ),
        in_specs=[
            anywhere, pl.BlockSpec(memory_space=pltpu.SMEM), anywhere, anywhere, anywhere, anywhere,
        ],
        out_specs=(vmem, vmem, vmem, vmem, vmem),
        scratch_shapes=[
            pltpu.VMEM((frames, feature), BF16),
            pltpu.VMEM((frames, feature), BF16),
            pltpu.VMEM((taps, 1, feature), F32),
            pltpu.VMEM((1, feature), F32),
            pltpu.VMEM((feature, feature), BF16),
            pltpu.VMEM((feature, feature), BF16),
            pltpu.VMEM(blocks, BF16),
            pltpu.VMEM(blocks, BF16),
            pltpu.VMEM((n_block + 1, BLOCK, feature), F32),
            pltpu.VMEM(blocks, F32),
            pltpu.VMEM(blocks, BF16),
            pltpu.VMEM((n_block, BLOCK, 128), F32),
            pltpu.VMEM(blocks, BF16),
            pltpu.VMEM(blocks, BF16),
            pltpu.VMEM(blocks, BF16),
            pltpu.VMEM((n_block + 1, BLOCK, feature), F32),
            pltpu.VMEM((BLOCK, feature), F32),
            pltpu.VMEM((taps, 8, feature), F32),
            pltpu.VMEM((taps, 8, feature), F32),
            pltpu.VMEM((8, feature), F32),
            pltpu.VMEM(own, BF16),
            pltpu.VMEM(own, BF16),
            pltpu.VMEM(own, BF16),
            pltpu.VMEM(own, BF16),
            pltpu.VMEM((3, n_block, BLOCK, feature // 2), BF16),
            pltpu.VMEM((3, n_block, BLOCK, feature // 2), BF16),
            pltpu.VMEM((RING, 2 * rows_own, feature // 2), F32),
            pltpu.VMEM((4 * HALF, 2 * rows_own, feature // 4), BF16),
            pltpu.VMEM((4 * HALF, 2 * rows_own, feature // 4), BF16),
            pltpu.VMEM((2, rows_own, feature // 2), F32),
            pltpu.VMEM((rows_own, feature // 2), BF16),
            pltpu.VMEM((rows_own, feature // 2), BF16),
            pltpu.VMEM((taps + 1, feature), BF16),
            pltpu.VMEM((taps + 1, feature // 2), BF16),
            pltpu.VMEM((taps + 1, feature // 2), BF16),
            pltpu.VMEM((taps + 1, feature // 4), BF16),
            pltpu.VMEM((RING, taps + 1, feature // 4), BF16),
            pltpu.VMEM((taps + 1, feature // 2), BF16),
            pltpu.VMEM((taps + 1, feature // 2), BF16),
            pltpu.VMEM((taps + 1, feature), F32),
            pltpu.SemaphoreType.DMA,
            pltpu.SemaphoreType.DMA((4,)),
            pltpu.SemaphoreType.DMA((n_block,)),
            pltpu.SemaphoreType.DMA((n_block,)),
            pltpu.SemaphoreType.DMA((n_block,)),
            pltpu.SemaphoreType.DMA((n_block,)),
            pltpu.SemaphoreType.DMA,
            pltpu.SemaphoreType.DMA,
            pltpu.SemaphoreType.DMA((per,)),
            pltpu.SemaphoreType.DMA((per,)),
            pltpu.SemaphoreType.DMA,
            pltpu.SemaphoreType.DMA((3,)),
            pltpu.SemaphoreType.DMA,
            pltpu.SemaphoreType.DMA((3,)),
            pltpu.SemaphoreType.DMA((4 * HALF,)),
            pltpu.SemaphoreType.DMA((4 * HALF,)),
            pltpu.SemaphoreType.DMA((2,)),
            pltpu.SemaphoreType.DMA((5,)),
            pltpu.SemaphoreType.DMA((5,)),
        ],
        compiler_params=pltpu.CompilerParams(
            collective_id=0, has_side_effects=True, vmem_limit_bytes=60 * 1024 * 1024
        ),
        cost_estimate=pl.CostEstimate(
            flops=6 * n_block * BLOCK * feature * feature, bytes_accessed=4 * feature * feature, transcendentals=0
        ),
    )(x, lengths, cot, weight, kern, gain)


def hand_over(*refs):
    count = len(refs) // 2
    for taken, given in zip(refs[:count], refs[count:]):
        given[...] = taken[...]


def local(inputs, lengths, cotangent, weight, kern, gain):
    results = pipeline(inputs[0], lengths, cotangent[0], weight[0], jnp.transpose(kern, (1, 0, 2)), gain)
    vmem = pl.BlockSpec(memory_space=pltpu.VMEM)
    out, igrad, wg, kgrad, ggrad = pl.pallas_call(
        hand_over,
        out_shape=tuple(jax.ShapeDtypeStruct(r.shape, r.dtype) for r in results),
        in_specs=[vmem] * len(results),
        out_specs=(vmem,) * len(results),
    )(*results)
    return (out[None], igrad[None], wg[None], jnp.transpose(kgrad, (1, 0, 2)), ggrad)


def solution(mesh):
    return jax.shard_map(
        local,
        mesh=mesh,
        in_specs=(
            P("dp", "section", None),
            P("dp"),
            P("dp", "section", None),
            P("section", None, None),
            P("section", None, None),
            P("section", None),
        ),
        out_specs=(
            P("dp", "section", None),
            P("dp", "section", None),
            P("section", "dp", None),
            P("section", None, None),
            P("section", None),
        ),
        check_vma=False,
    )
```
